128 devices in a mesh: dp: 16 (over z_hi, x, core), seq: 8 (over y, z_lo).
Axes of the slice: x: 4, y: 4, z: 4 (z_hi: 2, z_lo: 2; z = z_hi * 2 + z_lo), core: 2. Of those that a mesh axis runs over, the one named last changes fastest.
Arguments:
- tokens: bfloat16 [1024, 16, 1024], P('seq', 'dp'), may hold values from -6 to 6
- cotangent: bfloat16 [1024, 16, 1024], P('seq', 'dp'), may hold values from -6 to 6
- lengths: int32 [16, 4], P('dp'), may hold values from 1 to 1021, as said below
- w_qkv: float32 [2, 1024, 3072], P(None, ('dp', 'seq')), may hold values from -0.1875 to 0.1875
- w_out: float32 [2, 1024, 1024], P(None, ('dp', 'seq')), may hold values from -0.1875 to 0.1875
- w_up: float32 [2, 1024, 4096], P(None, ('dp', 'seq')), may hold values from -0.1875 to 0.1875
- w_down: float32 [2, 4096, 1024], P(None, ('dp', 'seq')), may hold values from -0.09375 to 0.09375
- gains: float32 [2, 4, 1024], P(None, None, ('dp', 'seq')), may hold values from 0.5 to 1.5
- moment_qkv: float32 [2, 1024, 3072], P(None, ('dp', 'seq')), may hold values from -64 to 64
- moment_out: float32 [2, 1024, 1024], P(None, ('dp', 'seq')), may hold values from -64 to 64
- moment_up: float32 [2, 1024, 4096], P(None, ('dp', 'seq')), may hold values from -64 to 64
- moment_down: float32 [2, 4096, 1024], P(None, ('dp', 'seq')), may hold values from -64 to 64
- moment_gains: float32 [2, 4, 1024], P(None, None, ('dp', 'seq')), may hold values from -64 to 64
- square_qkv: float32 [2, 1024, 3072], P(None, ('dp', 'seq')), may hold values from 327.68 to 3276.8
- square_out: float32 [2, 1024, 1024], P(None, ('dp', 'seq')), may hold values from 327.68 to 3276.8
- square_up: float32 [2, 1024, 4096], P(None, ('dp', 'seq')), may hold values from 327.68 to 3276.8
- square_down: float32 [2, 4096, 1024], P(None, ('dp', 'seq')), may hold values from 327.68 to 3276.8
- square_gains: float32 [2, 4, 1024], P(None, None, ('dp', 'seq')), may hold values from 327.68 to 3276.8
Outputs:
- output: bfloat16 [1024, 16, 1024], P('seq', 'dp')
- input_grad: bfloat16 [1024, 16, 1024], P('seq', 'dp')
- new_qkv: float32 [2, 1024, 3072], P(None, ('dp', 'seq'))
- new_out: float32 [2, 1024, 1024], P(None, ('dp', 'seq'))
- new_up: float32 [2, 1024, 4096], P(None, ('dp', 'seq'))
- new_down: float32 [2, 4096, 1024], P(None, ('dp', 'seq'))
- new_gains: float32 [2, 4, 1024], P(None, None, ('dp', 'seq'))
- next_moment_qkv: float32 [2, 1024, 3072], P(None, ('dp', 'seq'))
- next_moment_out: float32 [2, 1024, 1024], P(None, ('dp', 'seq'))
- next_moment_up: float32 [2, 1024, 4096], P(None, ('dp', 'seq'))
- next_moment_down: float32 [2, 4096, 1024], P(None, ('dp', 'seq'))
- next_moment_gains: float32 [2, 4, 1024], P(None, None, ('dp', 'seq'))
- next_square_qkv: float32 [2, 1024, 3072], P(None, ('dp', 'seq'))
- next_square_out: float32 [2, 1024, 1024], P(None, ('dp', 'seq'))
- next_square_up: float32 [2, 1024, 4096], P(None, ('dp', 'seq'))
- next_square_down: float32 [2, 4096, 1024], P(None, ('dp', 'seq'))
- next_square_gains: float32 [2, 4, 1024], P(None, None, ('dp', 'seq'))
- copy_qkv: bfloat16 [2, 1024, 3072], P(None, ('dp', 'seq'))
- copy_out: bfloat16 [2, 1024, 1024], P(None, ('dp', 'seq'))
- copy_up: bfloat16 [2, 1024, 4096], P(None, ('dp', 'seq'))
- copy_down: bfloat16 [2, 4096, 1024], P(None, ('dp', 'seq'))
- copy_gains: bfloat16 [2, 4, 1024], P(None, None, ('dp', 'seq'))
The draws below stay inside these ranges and needn't reach their ends.
Inputs may be any that keep to these rules, and one draw needn't show every extreme that they name: Each row's 4 document lengths are positive and sum to 1024.
All inputs are finite; a program needn't handle non-finite values.
Results may differ from the reference program's by a relative error of at most 0.025.
Values may be sent and summed in bfloat16 or wider, within the bound.
No kernel may reach another device: no remote copies, remote signals or barrier semaphores. Data moves between devices by JAX's collectives and lax.ppermute only.
A program may use at most 256 MiB of HBM per device.

```python
import math
import jax
import jax.numpy as jnp
from jax import lax

D = 1024
HEADS = 16
HEAD_DIM = 64
FF = 4096
LAYERS = 2
STEP = 5
LENGTH = 1024
BLOCK = 128
ROWS = 16
TOKENS = 16384


def draw_lengths(key, part):
    key = jax.random.fold_in(key, 7)
    key_one, key_two, key_three = jax.random.split(key, 3)
    leading = jax.random.randint(key_one, (ROWS, 1), 1, BLOCK)
    third_doc = jax.random.randint(key_two, (ROWS, 1), 1, BLOCK // 2)
    fourth_doc = jax.random.randint(key_three, (ROWS, 1), 1, BLOCK // 2)
    spanning = LENGTH - leading - third_doc - fourth_doc
    return jnp.concatenate([leading, spanning, third_doc, fourth_doc], axis=1).astype(jnp.int32)


def level_of(stream_key, dims, cuts, least, high):
    def one(dim, parts):
        steps = jax.random.uniform(jax.random.fold_in(jax.random.fold_in(stream_key, 6), dim), (parts,), jnp.float32, least / len(cuts), high / len(cuts))
        return jnp.repeat(jnp.exp(steps), dims[dim] // parts).reshape((-1,) + (1,) * (len(dims) - dim - 1))

    loudness = one(*cuts[0])
    for cut in cuts[1:]:
        loudness = loudness * one(*cut)
    return loudness


def centred(rng, extent, scale, reach, shards=(), kind=jnp.bfloat16):
    array = jax.random.normal(rng, extent, jnp.float32) * scale
    if len(shards) > 0:
        array = level_of(rng, extent, shards, -0.22, 0.18) * array
    return jnp.clip(array, min=-reach, max=reach).astype(kind)


def setup_inputs(seed: int = 0) -> dict:
    keys = jax.random.split(jax.random.key(seed), 19)
    tokens = centred(keys[0], (LENGTH, ROWS, D), 1.0, 6.0, ((0, 8), (1, 16)))
    cotangent = centred(keys[1], (LENGTH, ROWS, D), 1.0, 6.0, ((0, 8), (1, 16)))
    lengths = draw_lengths(jax.random.fold_in(keys[18], 71), 0)
    w_qkv = centred(keys[3], (LAYERS, D, 3 * D), D ** -0.5, 0.1875, ((1, 128),), jnp.float32)
    w_out = centred(keys[4], (LAYERS, D, D), D ** -0.5, 0.1875, ((1, 128),), jnp.float32)
    w_up = centred(keys[5], (LAYERS, D, FF), D ** -0.5, 0.1875, ((1, 128),), jnp.float32)
    w_down = centred(keys[6], (LAYERS, FF, D), FF ** -0.5, 0.09375, ((1, 128),), jnp.float32)
    gains = jnp.clip(1.0 + 0.1 * jax.random.normal(keys[7], (LAYERS, 4, D), jnp.float32), 0.5, 1.5)
    moment_qkv = centred(keys[8], (LAYERS, D, 3 * D), (0.08 * TOKENS ** 0.5), 64.0, ((1, 128),), jnp.float32)
    moment_out = centred(keys[9], (LAYERS, D, D), (0.08 * TOKENS ** 0.5), 64.0, ((1, 128),), jnp.float32)
    moment_up = centred(keys[10], (LAYERS, D, FF), (0.08 * TOKENS ** 0.5), 64.0, ((1, 128),), jnp.float32)
    moment_down = centred(keys[11], (LAYERS, FF, D), (0.08 * TOKENS ** 0.5), 64.0, ((1, 128),), jnp.float32)
    moment_gains = centred(keys[12], (LAYERS, 4, D), (0.08 * TOKENS ** 0.5), 64.0, ((2, 128),), jnp.float32)
    square_qkv = jnp.clip(jnp.exp(math.log(3276.8) - 2.3025851 * jax.random.uniform(keys[13], (LAYERS, D, 3 * D), jnp.float32) ** level_of(keys[13], (LAYERS, D, 3 * D), ((1, 128),), -0.2, 0.2)), 327.68, 3276.8)
    square_out = jnp.clip(jnp.exp(math.log(3276.8) - 2.3025851 * jax.random.uniform(keys[14], (LAYERS, D, D), jnp.float32) ** level_of(keys[14], (LAYERS, D, D), ((1, 128),), -0.2, 0.2)), 327.68, 3276.8)
    square_up = jnp.clip(jnp.exp(math.log(3276.8) - 2.3025851 * jax.random.uniform(keys[15], (LAYERS, D, FF), jnp.float32) ** level_of(keys[15], (LAYERS, D, FF), ((1, 128),), -0.2, 0.2)), 327.68, 3276.8)
    square_down = jnp.clip(jnp.exp(math.log(3276.8) - 2.3025851 * jax.random.uniform(keys[16], (LAYERS, FF, D), jnp.float32) ** level_of(keys[16], (LAYERS, FF, D), ((1, 128),), -0.2, 0.2)), 327.68, 3276.8)
    square_gains = jnp.clip(jnp.exp(math.log(3276.8) - 2.3025851 * jax.random.uniform(keys[17], (LAYERS, 4, D), jnp.float32) ** level_of(keys[17], (LAYERS, 4, D), ((2, 128),), -0.2, 0.2)), 327.68, 3276.8)
    return {"tokens": tokens, "cotangent": cotangent, "lengths": lengths, "w_qkv": w_qkv, "w_out": w_out, "w_up": w_up, "w_down": w_down, "gains": gains, "moment_qkv": moment_qkv, "moment_out": moment_out, "moment_up": moment_up, "moment_down": moment_down, "moment_gains": moment_gains, "square_qkv": square_qkv, "square_out": square_out, "square_up": square_up, "square_down": square_down, "square_gains": square_gains}


@jax.custom_vjp
def low(v):
    return lax.optimization_barrier(v.astype(jnp.bfloat16)).astype(jnp.float32)

@jax.custom_vjp
def low_back(v):
    return v

def low_keep(v):
    return (low(v), None)

def low_pass(kept, grad):
    return (grad,)

def back_keep(v):
    return (v, None)

def back_low(kept, grad):
    return (low(grad),)
low.defvjp(low_keep, low_pass)
low_back.defvjp(back_keep, back_low)
norm_eps = 1e-05
beta_first = 0.9
beta_second = 0.95
adam_eps = 1e-08
weight_decay = 0.1
rate_matrix = 0.04
rate_gain = 0.4
masked_score = -1e+30
highest = lax.Precision.HIGHEST

def rms_norm(values, gain_row):
    scaled = lax.rsqrt(lax.optimization_barrier(jnp.mean(values * values, axis=-1, keepdims=True)) + norm_eps)
    return values * scaled * gain_row

def rotate(values, cosine, sine_table):
    half_dim = values.shape[-1] // 2
    first_half = values[..., :half_dim]
    second_half = values[..., half_dim:]
    return jnp.concatenate([first_half * cosine - second_half * sine_table, second_half * cosine + first_half * sine_table], axis=-1)

def rotary_tables(positions):
    half_dim = HEAD_DIM // 2
    inverse = 10000.0 ** (-jnp.arange(half_dim, dtype=jnp.float32) / half_dim)
    angle = positions.astype(jnp.float32)[..., None] * inverse
    return (jnp.cos(angle), jnp.sin(angle))

def doc_tables(lengths, length_total):
    ends = jnp.cumsum(lengths, axis=-1).astype(jnp.int32)
    starts = (ends - lengths).astype(jnp.int32)
    places = jnp.arange(length_total, dtype=jnp.int32)
    doc_ids = lax.optimization_barrier(jnp.sum((places[None, :, None] >= ends[:, None, :]).astype(jnp.int32), axis=-1)).astype(jnp.int32)
    picked = doc_ids[:, :, None] == jnp.arange(lengths.shape[-1], dtype=jnp.int32)[None, None, :]
    first_place = lax.optimization_barrier(jnp.sum(jnp.where(picked, starts[:, None, :], 0), axis=-1)).astype(jnp.int32)
    return (doc_ids, (places[None, :] - first_place).astype(jnp.int32))

def adam_update(master, moment_one, moment_two, gradient, rate, decay):
    moment_new = beta_first * moment_one + (1.0 - beta_first) * gradient
    square_new = beta_second * moment_two + (1.0 - beta_second) * gradient * gradient
    moment_hat = moment_new / (1.0 - beta_first ** STEP)
    square_hat = square_new / (1.0 - beta_second ** STEP)
    updated = master - rate * (moment_hat / (jnp.sqrt(square_hat) + adam_eps) + decay * master)
    return (updated, moment_new, square_new)

def layer_forward(hidden, lowered, layer_index, row_docs, cosine, sine_table):
    weight_qkv = lowered[0][layer_index]
    weight_out = lowered[1][layer_index]
    weight_up = lowered[2][layer_index]
    weight_down = lowered[3][layer_index]
    gain_rows = lowered[4][layer_index]
    normed = rms_norm(hidden, gain_rows[0])
    mixed_qkv = low_back(jnp.dot(low(normed), weight_qkv, precision=highest, preferred_element_type=jnp.float32))
    qkv_parts = mixed_qkv.reshape(LENGTH, 3, HEADS, HEAD_DIM)
    queries = low(rotate(qkv_parts[:, 0], cosine, sine_table))
    key_all = low(rotate(qkv_parts[:, 1], cosine, sine_table))
    value_all = low(qkv_parts[:, 2])
    places = jnp.arange(LENGTH, dtype=jnp.int32)
    allowed = (row_docs[:, None] == row_docs[None, :]) & (places[None, :] <= places[:, None])
    scores = low_back(jnp.einsum('qhd,khd->hqk', queries, key_all, precision=highest) * HEAD_DIM ** (-0.5))
    masked = jnp.where(allowed[None], scores, masked_score)
    largest = lax.optimization_barrier(jnp.max(masked, axis=-1, keepdims=True))
    exponent = jnp.exp(masked - largest)
    probabilities = exponent / lax.optimization_barrier(jnp.sum(exponent, axis=-1, keepdims=True))
    attended = jnp.einsum('hqk,khd->qhd', low(probabilities), value_all, precision=highest).reshape(LENGTH, D)
    attended = low_back(low(attended))
    branch = low_back(jnp.dot(attended, weight_out, precision=highest, preferred_element_type=jnp.float32))
    middle = hidden + rms_norm(branch, gain_rows[1])
    upward = low_back(jnp.dot(low(rms_norm(middle, gain_rows[2])), weight_up, precision=highest, preferred_element_type=jnp.float32))
    active = low(jax.nn.gelu(upward, approximate=False))
    downward = low_back(jnp.dot(active, weight_down, precision=highest, preferred_element_type=jnp.float32))
    return middle + rms_norm(downward, gain_rows[3])

def reference(tokens, cotangent, lengths, w_qkv, w_out, w_up, w_down, gains, moment_qkv, moment_out, moment_up, moment_down, moment_gains, square_qkv, square_out, square_up, square_down, square_gains):
    doc_ids, positions = doc_tables(lengths, LENGTH)
    cosine, sine_table = rotary_tables(positions)

    def forward(inputs, master_qkv, master_out, master_up, master_down, master_gains):
        lowered = (low(master_qkv), low(master_out), low(master_up), low(master_down), low(master_gains))

        def one_row(row_inputs):
            hidden, row_docs, row_cosine, row_sine = row_inputs
            for layer_index in range(LAYERS):
                hidden = layer_forward(hidden, lowered, layer_index, row_docs, row_cosine[:, None, :], row_sine[:, None, :])
            return hidden
        results = lax.map(jax.checkpoint(one_row), (jnp.transpose(inputs, (1, 0, 2)), doc_ids, cosine, sine_table))
        return jnp.transpose(results, (1, 0, 2))
    result_out, pullback = jax.vjp(forward, tokens.astype(jnp.float32), w_qkv, w_out, w_up, w_down, gains)
    gradients = pullback(cotangent.astype(jnp.float32))
    upd_qkv = adam_update(w_qkv, moment_qkv, square_qkv, gradients[1], rate_matrix, weight_decay)
    upd_out = adam_update(w_out, moment_out, square_out, gradients[2], rate_matrix, weight_decay)
    upd_up = adam_update(w_up, moment_up, square_up, gradients[3], rate_matrix, weight_decay)
    upd_down = adam_update(w_down, moment_down, square_down, gradients[4], rate_matrix, weight_decay)
    upd_gains = adam_update(gains, moment_gains, square_gains, gradients[5], rate_gain, 0.0)
    return (result_out.astype(jnp.bfloat16), gradients[0].astype(jnp.bfloat16), upd_qkv[0], upd_out[0], upd_up[0], upd_down[0], upd_gains[0], upd_qkv[1], upd_out[1], upd_up[1], upd_down[1], upd_gains[1], upd_qkv[2], upd_out[2], upd_up[2], upd_down[2], upd_gains[2], upd_qkv[0].astype(jnp.bfloat16), upd_out[0].astype(jnp.bfloat16), upd_up[0].astype(jnp.bfloat16), upd_down[0].astype(jnp.bfloat16), upd_gains[0].astype(jnp.bfloat16))
```

```python
import jax
import jax.numpy as jnp
from jax import lax
from jax.experimental import pallas as pl
from jax.experimental.pallas import tpu as pltpu
from jax.sharding import Mesh
from jax.sharding import PartitionSpec as P

D = 1024
HEADS = 16
HEAD_DIM = 64
FF = 4096
LAYERS = 2
STEP = 5
LENGTH = 1024
BLOCK = 128
QB = 256

norm_eps = 1e-05
beta_first = 0.9
beta_second = 0.95
adam_eps = 1e-08
weight_decay = 0.1
rate_matrix = 0.04
rate_gain = 0.4
masked_score = -1e30
score_scale = HEAD_DIM ** (-0.5)

bf16 = jnp.bfloat16
f32 = jnp.float32
SEQ = ("y", "zl")
DP = ("zh", "x", "c")
ZAX = ("zh", "zl")
XY = ("x", "y")
ALL = ("zh", "x", "c", "y", "zl")


def dot(a, b, dims):
    return lax.dot_general(a, b, (dims, ((), ())), preferred_element_type=f32)


def mm(a, b):
    return dot(a, b, ((1,), (0,)))


def mm_nt(a, b):
    return dot(a, b, ((1,), (1,)))


def mm_tn(a, b):
    return dot(a, b, ((0,), (0,)))


def swap_halves(x):
    lane = lax.broadcasted_iota(jnp.int32, x.shape, 1)
    return jnp.where((lane % 64) < 32, pltpu.roll(x, 96, 1), pltpu.roll(x, 32, 1))


def lane_mask(x, row):
    lane = lax.broadcasted_iota(jnp.int32, x.shape, 1)
    return jnp.where((lane // 64) == row, x, jnp.zeros_like(x))


def allowed_mask(start_row, keys, first_query):
    key = lax.broadcasted_iota(jnp.int32, (keys, QB), 0)
    query = lax.broadcasted_iota(jnp.int32, (keys, QB), 1) + first_query
    return (key >= start_row) & (key <= query)


def att_fwd_kernel(qkv_ref, cos_ref, sin_ref, start_ref, att_ref, lse_ref, rot_ref, att_t):
    cosine = cos_ref[...]
    sine = sin_ref[...]
    q = qkv_ref[:, 0:128].astype(f32)
    k = qkv_ref[:, 128:256].astype(f32)
    v = qkv_ref[:, 256:384]
    q = q * cosine + swap_halves(q) * sine
    k = k * cosine + swap_halves(k) * sine
    rot_ref[:, 0:128] = q.astype(bf16)
    rot_ref[:, 128:256] = k.astype(bf16)
    rot_ref[:, 256:384] = v
    v_t = jnp.transpose(v.astype(f32)).astype(bf16)
    for row in range(2):
        k_row = lane_mask(k, row).astype(bf16)
        for step in range(LENGTH // QB):
            first = step * QB
            keys = first + QB
            q_blk = rot_ref[first : first + QB, 0:128]
            s = mm_nt(k_row[:keys], q_blk) * score_scale
            ok = allowed_mask(start_ref[row : row + 1, first : first + QB], keys, first)
            s = jnp.where(ok, s, masked_score)
            top = jnp.max(s, axis=0, keepdims=True)
            e = jnp.exp(s - top)
            total = jnp.sum(e, axis=0, keepdims=True)
            lse_ref[row : row + 1, first : first + QB] = top + jnp.log(total)
            p = (e * (1.0 / total)).astype(bf16)
            att_t[row * 64 : row * 64 + 64, first : first + QB] = mm(
                v_t[row * 64 : row * 64 + 64, :keys], p
            )
    att_ref[...] = jnp.transpose(att_t[...]).astype(bf16)


def att_bwd_kernel(rot_ref, datt_ref, lse_ref, cos_ref, sin_ref, start_ref, out_ref, dk_acc, dv_acc, dq_t):
    cosine = cos_ref[...]
    sine = sin_ref[...]
    q = rot_ref[:, 0:128]
    k = rot_ref[:, 128:256]
    v = rot_ref[:, 256:384]
    datt = datt_ref[...]
    k_t = jnp.transpose(k.astype(f32)).astype(bf16)
    dk_acc[...] = jnp.zeros_like(dk_acc)
    dv_acc[...] = jnp.zeros_like(dv_acc)
    for row in range(2):
        q_row = lane_mask(q, row)
        datt_row = lane_mask(datt, row)
        for step in range(LENGTH // QB):
            first = step * QB
            keys = first + QB
            q_blk = q_row[first : first + QB]
            datt_blk = datt_row[first : first + QB]
            s = mm_nt(k[:keys], q_blk) * score_scale
            ok = allowed_mask(start_ref[row : row + 1, first : first + QB], keys, first)
            p = jnp.where(ok, jnp.exp(s - lse_ref[row : row + 1, first : first + QB]), 0.0)
            dp = mm_nt(v[:keys], datt_blk)
            delta = jnp.sum(p * dp, axis=0, keepdims=True)
            ds = (p * (dp - delta)).astype(bf16)
            dq_t[row * 64 : row * 64 + 64, first : first + QB] = mm(
                k_t[row * 64 : row * 64 + 64, :keys], ds
            )
            dk_acc[0:keys, :] += mm(ds, q_blk)
            dv_acc[0:keys, :] += mm(p.astype(bf16), datt_blk)
    dq = jnp.transpose(dq_t[...]) * score_scale
    dk = dk_acc[...] * score_scale
    out_ref[:, 0:128] = (dq * cosine - swap_halves(dq) * sine).astype(bf16)
    out_ref[:, 128:256] = (dk * cosine - swap_halves(dk) * sine).astype(bf16)
    out_ref[:, 256:384] = dv_acc[...].astype(bf16)


def whole(count):
    return [pl.BlockSpec(memory_space=pltpu.VMEM)] * count


def att_forward(qkv, cosine, sine, starts):
    return pl.pallas_call(
        att_fwd_kernel,
        out_shape=(
            jax.ShapeDtypeStruct((LENGTH, 128), bf16),
            jax.ShapeDtypeStruct((8, LENGTH), f32),
            jax.ShapeDtypeStruct((LENGTH, 384), bf16),
        ),
        in_specs=whole(4),
        out_specs=tuple(whole(3)),
        scratch_shapes=[pltpu.VMEM((128, LENGTH), f32)],
        compiler_params=pltpu.CompilerParams(vmem_limit_bytes=16 * 1024 * 1024),
        name="att_forward",
    )(qkv, cosine, sine, starts)


def att_backward(rot, datt, lse, cosine, sine, starts):
    return pl.pallas_call(
        att_bwd_kernel,
        out_shape=jax.ShapeDtypeStruct((LENGTH, 384), bf16),
        in_specs=whole(6),
        out_specs=whole(1)[0],
        scratch_shapes=[
            pltpu.VMEM((LENGTH, 128), f32),
            pltpu.VMEM((LENGTH, 128), f32),
            pltpu.VMEM((128, LENGTH), f32),
        ],
        compiler_params=pltpu.CompilerParams(vmem_limit_bytes=16 * 1024 * 1024),
        name="att_backward",
    )(rot, datt, lse, cosine, sine, starts)


def rms_scale(values):
    return lax.rsqrt(jnp.mean(values * values, axis=-1, keepdims=True) + norm_eps)


def rms_norm(values, gain_row):
    return values * rms_scale(values) * gain_row


def rms_back(values, gain_row, grad):
    scale = rms_scale(values)
    unit = values * scale
    scaled = grad * gain_row
    inner = jnp.mean(scaled * unit, axis=-1, keepdims=True)
    return scale * (scaled - unit * inner), jnp.sum(grad * unit, axis=0)


def adam_update(master, moment_one, moment_two, gradient, rate, decay):
    moment_new = beta_first * moment_one + (1.0 - beta_first) * gradient
    square_new = beta_second * moment_two + (1.0 - beta_second) * gradient * gradient
    moment_hat = moment_new / (1.0 - beta_first**STEP)
    square_hat = square_new / (1.0 - beta_second**STEP)
    updated = master - rate * (moment_hat / (jnp.sqrt(square_hat) + adam_eps) + decay * master)
    return (updated, moment_new, square_new)


def other_core(x):
    return lax.ppermute(x, "c", [(0, 1), (1, 0)])


def both_rows(x):
    return jnp.concatenate([x, other_core(x)], axis=0)


def own_sum(part):
    sent = other_core(part[BLOCK:].astype(bf16))
    return part[:BLOCK] + sent.astype(f32)


def seq_swap(x):
    return lax.all_to_all(x, SEQ, 0, 0, tiled=True)


CUBE, PLANE, LINE = 0, 3, 4
QKV, OUT, UP, DOWN, GAIN = "qkv", "out", "up", "down", "gain"
WIDTH = {QKV: 1536, OUT: 512, UP: 2048, DOWN: 2048, GAIN: 128}
SHAPE = {QKV: (1024, 1536), OUT: (512, 1024), UP: (1024, 2048), DOWN: (2048, 1024), GAIN: (1024, 128)}


def place(i):
    return (i // 64) * 2 + i % 2, (i // 16) % 4, (i // 8) % 2, (i // 2) % 4


def device_at(z, x, c, y):
    return (((z // 2) * 4 + x) * 2 + c) * 8 + y * 2 + z % 2


def pairs(axis, phase):
    found = []
    for i in range(128):
        z, x, c, y = place(i)
        mask = 3 if (c if phase else 1 - c) else 1
        x, y, z = (x ^ mask, y, z) if axis == 0 else (x, y ^ mask, z) if axis == 1 else (x, y, z ^ mask)
        found.append((i, device_at(z, x, c, y)))
    return found


PAIRS = {(axis, phase): pairs(axis, phase) for axis in range(3) for phase in range(2)}


def pair_swap(x, axis, phase):
    return lax.ppermute(x, ALL, PAIRS[axis, phase])


def add_low(a, b):
    return (a.astype(f32) + b.astype(f32)).astype(bf16)


def cube_groups():
    found = {}
    for i in range(128):
        z, x, c, y = place(i)
        shift, mask = (0, 1) if c else (1, 3)
        rank = ((x >> shift) & 1) * 4 + ((y >> shift) & 1) * 2 + ((z >> shift) & 1)
        key = (c,) + tuple(min(v, v ^ mask) for v in (x, y, z))
        found.setdefault(key, [0] * 8)[rank] = i
    return list(found.values())


CUBES = cube_groups()


def cube_all_to_all(x):
    return lax.all_to_all(x, ALL, 0, 0, axis_index_groups=CUBES, tiled=True)


def cube_round(cur, k):
    return [pair_swap(cur[g], (g + k) % 3, 1) for g in range(3)]


def join(cur, got):
    return [jnp.concatenate([x, y], axis=0) for x, y in zip(cur, got)]


def scatter_round(keep, send, k):
    cur = [add_low(x, y) for x, y in zip(keep, cube_round(send, k))]
    half = cur[0].shape[0] // 2
    return [x[:half] for x in cur], [x[half:] for x in cur]


def together(*values):
    return lax.optimization_barrier(values)


def unit_tables(mine):
    my_z, my_x, core, my_y = mine
    first = jnp.where(core == 0, 3, 1)
    last = jnp.where(core == 0, 1, 3)
    shift = jnp.where(core == 0, 1, 0)
    p = jnp.arange(64, dtype=jnp.int32)
    rows = []
    for g in range(5):
        if g < 3:
            at = [my_x, my_y, my_z]
            for k in range(3):
                at[(g + k) % 3] = at[(g + k) % 3] ^ (((p >> (3 + k)) & 1) * last)
            for axis in range(3):
                differs = ((at[axis] >> shift) & 1) ^ ((p >> (2 - axis)) & 1)
                at[axis] = at[axis] ^ (differs * first)
            x, y, z = at
        else:
            plane, line = (p >> 2, p & 3) if g == 3 else (p & 15, p >> 4)
            x, y = plane >> 2, plane & 3
            z = my_z ^ ((line & 1) * last) ^ ((line >> 1) * first)
        zh, zl = z >> 1, z & 1
        rows += [
            (((zh * 4 + x) * 2 + zl) * 4 + y) * 16,
            ((zh * 4 + x) * 4 + y) * 16,
            zl * 512,
            (((zh * 4 + x) * 4 + y) * 2 + zl) * 32,
        ]
    return jnp.stack(rows).astype(jnp.int32)


def segments(names, bounds):
    pieces = []
    start = 0
    for name in names:
        for part in range(2 if name == DOWN else 1):
            width = 1024 if name == DOWN else WIDTH[name]
            pieces.append((name, start, width, 16 * part))
            start += width
    found = []
    for a, b in bounds:
        group = []
        for name, first, width, extra in pieces:
            lo, hi = max(a, first), min(b, first + width)
            if lo < hi:
                group.append((name, lo - a, lo - first, hi - lo, extra))
        found.append(group)
    return found


def whole_slice(tab, ref, name, group, p, column, count, extra):
    if name == OUT:
        row = pl.multiple_of(tab[4 * group + 1, p], 16)
        col = pl.multiple_of(tab[4 * group + 2, p] + column, 128)
        return ref.at[pl.ds(row, 16), pl.ds(col, count)]
    if name == DOWN:
        row = pl.multiple_of(tab[4 * group + 3, p] + extra, 16)
    else:
        row = pl.multiple_of(tab[4 * group, p], 16)
    return ref.at[pl.ds(row, 16), pl.ds(column, count)]


def unpack(names, bounds, groups, tables, order):
    plan = segments(names, bounds)
    per = len(groups[0])
    flat = [buffer for group in groups for buffer in group]

    def kernel(tab, *refs):
        sources = refs[: len(flat)]
        targets = dict(zip(names, refs[len(flat) : len(flat) + len(names)]))
        sems = refs[-1]

        def step(i, carry):
            for g, group in enumerate(plan):
                for part in range(per):
                    for name, at, column, count, extra in group:
                        pltpu.make_async_copy(
                            sources[g * per + part].at[i, :, pl.ds(at, count)],
                            whole_slice(tab, targets[name], name, order + g, i + part * (64 // per), column, count, extra),
                            sems.at[names.index(name)],
                        ).start()
            return carry

        lax.fori_loop(0, 64 // per, step, 0)
        for n, name in enumerate(names):
            pltpu.make_async_copy(targets[name], targets[name], sems.at[n]).wait()

    return pl.pallas_call(
        kernel,
        out_shape=tuple(jax.ShapeDtypeStruct(SHAPE[name], bf16) for name in names),
        in_specs=[pl.BlockSpec(memory_space=pltpu.SMEM)] + [pl.BlockSpec(memory_space=pl.ANY)] * len(flat),
        out_specs=tuple(whole(len(names))),
        scratch_shapes=[pltpu.SemaphoreType.DMA((len(names),))],
        compiler_params=pltpu.CompilerParams(vmem_limit_bytes=20 * 1024 * 1024),
        name="unpack",
    )(tables, *flat)


def pack(names, bounds, weights, tables, order):
    plan = segments(names, bounds)
    per = 2 if order == CUBE else 1
    shapes = [(64 // per, 16, b - a) for a, b in bounds for _ in range(per)]

    def kernel(tab, *refs):
        sources = dict(zip(names, refs[: len(names)]))
        targets = refs[len(names) : len(names) + len(shapes)]
        sems = refs[-1]

        def step(i, carry):
            for g, group in enumerate(plan):
                for part in range(per):
                    for name, at, column, count, extra in group:
                        pltpu.make_async_copy(
                            whole_slice(tab, sources[name], name, order + g, i + part * (64 // per), column, count, extra),
                            targets[g * per + part].at[i, :, pl.ds(at, count)],
                            sems.at[g * per + part],
                        ).start()
            return carry

        lax.fori_loop(0, 64 // per, step, 0)
        for n in range(len(shapes)):
            pltpu.make_async_copy(targets[n], targets[n], sems.at[n]).wait()

    out = pl.pallas_call(
        kernel,
        out_shape=tuple(jax.ShapeDtypeStruct(shape, bf16) for shape in shapes),
        in_specs=[pl.BlockSpec(memory_space=pltpu.SMEM)] + whole(len(names)),
        out_specs=tuple([pl.BlockSpec(memory_space=pl.ANY)] * len(shapes)),
        scratch_shapes=[pltpu.SemaphoreType.DMA((len(shapes),))],
        compiler_params=pltpu.CompilerParams(vmem_limit_bytes=20 * 1024 * 1024),
        name="pack",
    )(tables, *weights)
    return [out[g * per : (g + 1) * per] for g in range(len(bounds))]


def plane_gather(space):
    cur = space[None]
    for phase in (1, 0):
        cur = jnp.concatenate([cur, pair_swap(cur, 2, phase)], axis=0)
    return lax.all_gather(cur, XY, axis=0, tiled=True)


def plane_scatter(buffer):
    cur = lax.psum_scatter(buffer.reshape(1024, -1), XY, scatter_dimension=0, tiled=True).reshape(4, 16, -1)
    for phase in (0, 1):
        half = cur.shape[0] // 2
        cur = add_low(cur[:half], pair_swap(cur[half:], 2, phase))
    return cur[0]


CROSS = {
    flip: [
        (device_at(z, x, c, y), device_at((z // 2) * 2 + c, x, (z % 2) ^ flip, y))
        for z in range(4)
        for x in range(4)
        for c in range(2)
        for y in range(4)
    ]
    for flip in range(2)
}
CROSS_BACK = {flip: [(b, a) for a, b in CROSS[flip]] for flip in range(2)}


def rows_to_units(halves, zl, core):
    near = lax.ppermute(jnp.where(zl == 0, halves[0], halves[1]), ALL, CROSS[0])
    far = lax.ppermute(jnp.where(zl == 0, halves[1], halves[0]), ALL, CROSS[1])
    return jnp.where(core == 0, jnp.concatenate([near, far], axis=0), jnp.concatenate([far, near], axis=0))


def units_to_rows(units, zl, core):
    near = lax.ppermute(jnp.where(core == 0, units[:8], units[8:]), ALL, CROSS_BACK[0])
    far = lax.ppermute(jnp.where(core == 0, units[8:], units[:8]), ALL, CROSS_BACK[1])
    return jnp.where(zl == 0, jnp.stack([near, far]), jnp.stack([far, near]))


def zl_swap(x):
    return lax.ppermute(x, "zl", [(0, 1), (1, 0)])


def out_to_unit(out, zl):
    low, high = out[..., :512], out[..., 512:]
    kept = jnp.where(zl == 0, low, high)
    got = zl_swap(jnp.where(zl == 0, high, low))
    return jnp.where(zl == 0, jnp.concatenate([kept, got], axis=1), jnp.concatenate([got, kept], axis=1))


def out_to_rows(units, zl):
    top, bottom = units[:, :8], units[:, 8:]
    kept = jnp.where(zl == 0, top, bottom)
    got = zl_swap(jnp.where(zl == 0, bottom, top))
    return jnp.where(zl == 0, jnp.concatenate([kept, got], axis=-1), jnp.concatenate([got, kept], axis=-1))


ATTN_NAMES = (QKV, OUT, GAIN)
ATTN_CUTS = ((0, 768), (768, 1536), (1536, 2176))
ZERO_NAMES = (QKV, OUT, GAIN, UP, DOWN)
ZERO_CUTS = ((0, 2176), (2176, 4224), (4224, 6272))
MLP_NAMES = (UP, DOWN)
LAYER_NAMES = (QKV, OUT, UP, DOWN)
LAYER_CUTS = ((0, 6144),)


def body(
    tokens,
    cotangent,
    lengths,
    w_qkv,
    w_out,
    w_up,
    w_down,
    gains,
    moment_qkv,
    moment_out,
    moment_up,
    moment_down,
    moment_gains,
    square_qkv,
    square_out,
    square_up,
    square_down,
    square_gains,
):
    core = lax.axis_index("c")
    zl = lax.axis_index("zl")
    my_z = lax.axis_index("zh") * 2 + zl
    tables = unit_tables((my_z, lax.axis_index("x"), core, lax.axis_index("y")))

    both = jnp.concatenate([lengths, other_core(lengths)], axis=0)
    ends = jnp.cumsum(both, axis=-1)
    starts = ends - both
    places = jnp.arange(LENGTH, dtype=jnp.int32)
    doc_ids = jnp.sum((places[None, :, None] >= ends[:, None, :]).astype(jnp.int32), axis=-1)
    picked = doc_ids[:, :, None] == jnp.arange(4, dtype=jnp.int32)[None, None, :]
    first_place = jnp.sum(jnp.where(picked, starts[:, None, :], 0), axis=-1)
    positions = (places[None, :] - first_place).astype(f32)
    inverse = 10000.0 ** (-jnp.arange(32, dtype=f32) / 32)
    angle = positions[:, :, None] * inverse
    cos_half = jnp.cos(angle)
    sin_half = jnp.sin(angle)
    cosine = jnp.concatenate([cos_half[0], cos_half[0], cos_half[1], cos_half[1]], axis=-1)
    sine = jnp.concatenate([-sin_half[0], sin_half[0], -sin_half[1], sin_half[1]], axis=-1)
    start_rows = jnp.concatenate([first_place, jnp.zeros((6, LENGTH), jnp.int32)], axis=0)

    qkv_halves = w_qkv.astype(bf16).reshape(LAYERS, 8, 3, 8, 2, 64).transpose(4, 1, 0, 3, 2, 5).reshape(2, 8, LAYERS * 1536)
    up_halves = w_up.astype(bf16).reshape(LAYERS, 8, 8, 2, 256).transpose(3, 1, 0, 2, 4).reshape(2, 8, LAYERS * 2048)
    gain_rows = gains.astype(bf16).reshape(8, 8).T
    gain_rows = jnp.broadcast_to(jnp.pad(gain_rows, ((0, 0), (0, 120)))[None], (2, 8, 128))
    units = rows_to_units(jnp.concatenate([qkv_halves, up_halves, gain_rows], axis=-1), zl, core)
    qkv_units, up_units, gain_units = units[:, :3072], units[:, 3072:7168], units[:, 7168:]
    out_units = out_to_unit(w_out.astype(bf16), zl)
    down_units = w_down.astype(bf16).reshape(LAYERS, 2, 16, 1024).transpose(0, 2, 1, 3).reshape(LAYERS, 16, 2048)
    attn_space = jnp.concatenate([qkv_units[:, :1536], out_units[0], gain_units], axis=-1)
    mlp_space = jnp.concatenate([up_units[:, :2048], down_units[0]], axis=-1)
    layer_space = jnp.concatenate([qkv_units[:, 1536:], out_units[1], up_units[:, 2048:], down_units[1]], axis=-1)
    zero_space = jnp.concatenate([attn_space, mlp_space], axis=-1)
    zero_space, cosine, sine, start_rows = together(zero_space, cosine, sine, start_rows)
    line = layer_space[None]
    line_got = pair_swap(line, 2, 1)
    eight = cube_all_to_all(jnp.broadcast_to(zero_space[None], (8,) + zero_space.shape))
    line, line_got, eight = together(line, line_got, eight)
    line = jnp.concatenate([line, line_got], axis=0)
    cur = [eight[..., a:b] for a, b in ZERO_CUTS]
    line, line_got, got = together(line, pair_swap(line, 2, 0), cube_round(cur, 0))
    line = jnp.concatenate([line, line_got], axis=0)
    cur = join(cur, got)
    cur = join(cur, cube_round(cur, 1))
    got = cube_round(cur, 2)
    line, got = together(line, got)
    layer_buffer = lax.all_gather(line, XY, axis=0, tiled=True)
    zero_groups = list(zip(cur, got))
    qkv_zero, out_zero, gain_whole, up_zero, down_zero = unpack(ZERO_NAMES, ZERO_CUTS, zero_groups, tables, CUBE)
    gain_all = gain_whole[:, :8].astype(f32).T.reshape(LAYERS, 4, D)

    hidden = tokens.reshape(BLOCK, D).astype(f32)
    kept = []
    for l in range(LAYERS):
        gain = gain_all[l]
        if l == 0:
            weight_qkv, weight_out, weight_up, weight_down = qkv_zero, out_zero, up_zero, down_zero
        else:
            weight_qkv, weight_out, weight_up, weight_down = unpack(
                LAYER_NAMES, LAYER_CUTS, [(layer_buffer,)], tables, PLANE
            )
        layer_input = hidden
        normed = both_rows(rms_norm(hidden, gain[0]).astype(bf16))
        mixed = mm(normed, weight_qkv).astype(bf16)
        mixed = mixed.reshape(2, BLOCK, 8, 3, 64).transpose(2, 1, 3, 0, 4).reshape(8, BLOCK, 384)
        mixed = seq_swap(mixed).reshape(LENGTH, 384)
        att_mine, lse, rot = att_forward(mixed, cosine, sine, start_rows)
        att = seq_swap(att_mine.reshape(8, BLOCK, 128))
        att = att.reshape(8, BLOCK, 2, 64).transpose(2, 1, 0, 3).reshape(2 * BLOCK, 512)
        branch = own_sum(mm(att, weight_out))
        middle = hidden + rms_norm(branch, gain[1])
        normed_mlp = both_rows(rms_norm(middle, gain[2]).astype(bf16))
        upward = mm(normed_mlp, weight_up)
        active = jax.nn.gelu(upward, approximate=False).astype(bf16)
        downward = own_sum(mm(active, weight_down))
        hidden = middle + rms_norm(downward, gain[3])
        kept.append(
            (
                layer_input,
                normed,
                rot,
                lse,
                att,
                branch,
                middle,
                normed_mlp,
                upward,
                active,
                downward,
                weight_qkv,
                weight_out,
                weight_up,
                weight_down,
            )
        )
    output = hidden.astype(bf16)

    grad_hidden = cotangent.reshape(BLOCK, D).astype(f32)
    gain_grads = [None] * LAYERS
    for l in reversed(range(LAYERS)):
        (
            layer_input,
            normed,
            rot,
            lse,
            att,
            branch,
            middle,
            normed_mlp,
            upward,
            active,
            downward,
            weight_qkv,
            weight_out,
            weight_up,
            weight_down,
        ) = kept[l]
        gain = gain_all[l]
        d_down, grad_three = rms_back(downward, gain[3], grad_hidden)
        d_down = both_rows(d_down.astype(bf16))
        d_active = mm_nt(d_down, weight_down)
        _, gelu_back = jax.vjp(lambda u: jax.nn.gelu(u, approximate=False), upward)
        d_up = gelu_back(d_active)[0].astype(bf16)
        d_normed = own_sum(mm_nt(d_up, weight_up))
        grad_wdown = mm_tn(active, d_down).astype(bf16)
        grad_wup = mm_tn(normed_mlp, d_up).astype(bf16)
        if l == 1:
            mlp_pack = pack(MLP_NAMES, ((0, 4096),), (grad_wup, grad_wdown), tables, PLANE)[0][0]
            mlp_pack, d_normed = together(mlp_pack, d_normed)
            mlp_own = plane_scatter(mlp_pack)
        else:
            mid_pack = pack(LAYER_NAMES, LAYER_CUTS, held + (grad_wup, grad_wdown), tables, PLANE)[0][0]
            mid_pack, d_normed = together(mid_pack, d_normed)
            mid_own = plane_scatter(mid_pack)
        d_middle, grad_two = rms_back(middle, gain[2], d_normed)
        d_middle = d_middle + grad_hidden
        d_branch, grad_one = rms_back(branch, gain[1], d_middle)
        d_branch = both_rows(d_branch.astype(bf16))
        d_att = mm_nt(d_branch, weight_out).astype(bf16)
        d_att = d_att.reshape(2, BLOCK, 8, 64).transpose(2, 1, 0, 3).reshape(8, BLOCK, 128)
        d_att = seq_swap(d_att).reshape(LENGTH, 128)
        grad_wout = mm_tn(att, d_branch).astype(bf16)
        d_mixed = att_backward(rot, d_att, lse, cosine, sine, start_rows)
        d_mixed = seq_swap(d_mixed.reshape(8, BLOCK, 384))
        d_mixed = d_mixed.reshape(8, BLOCK, 3, 2, 64).transpose(3, 1, 0, 2, 4).reshape(2 * BLOCK, 1536)
        grad_wqkv = mm_tn(normed, d_mixed).astype(bf16)
        held = (grad_wqkv, grad_wout)
        d_normed = own_sum(mm_nt(d_mixed, weight_qkv))
        d_input, grad_zero = rms_back(layer_input, gain[0], d_normed)
        grad_hidden = d_input + d_middle
        gain_grads[l] = jnp.stack([grad_zero, grad_one, grad_two, grad_three])
    input_grad = grad_hidden.astype(bf16)

    gain_sum = jnp.pad(jnp.stack(gain_grads).reshape(8, D).T.astype(bf16), ((0, 0), (0, 120)))
    tail_pack = pack(ATTN_NAMES, ATTN_CUTS, (grad_wqkv, grad_wout, gain_sum), tables, CUBE)
    tail = [x[0] for x in tail_pack], [x[1] for x in tail_pack]
    for k in (2, 1, 0):
        tail = scatter_round(*tail, k)
    tail_own = jnp.concatenate([jnp.concatenate(x, axis=-1) for x in tail], axis=0)
    tail_own = jnp.sum(cube_all_to_all(tail_own).astype(f32), axis=0).astype(bf16)

    g_out_units = jnp.stack([tail_own[:, 1536:2048], mid_own[:, 1536:2048]])
    g_down = jnp.stack([mid_own[:, 4096:], mlp_own[:, 2048:]])
    g_down = g_down.reshape(LAYERS, 16, 2, 1024).transpose(0, 2, 1, 3).reshape(LAYERS, 32, 1024).astype(f32)
    both = jnp.concatenate(
        [tail_own[:, :1536], mid_own[:, :1536], mid_own[:, 2048:4096], mlp_own[:, :2048], tail_own[:, 2048:]], axis=-1
    )
    both, g_out_units = together(both, g_out_units)
    g_out = out_to_rows(g_out_units, zl).astype(f32)
    both = units_to_rows(both, zl, core).astype(f32)
    g_qkv = both[..., :3072].reshape(2, 8, LAYERS, 8, 3, 64).transpose(2, 1, 4, 3, 0, 5).reshape(LAYERS, 8, 3 * D)
    g_up = both[..., 3072:7168].reshape(2, 8, LAYERS, 8, 256).transpose(2, 1, 3, 0, 4).reshape(LAYERS, 8, FF)
    g_gain = jnp.sum(both[:, :, 7168:7176], axis=0).T.reshape(LAYERS, 4, 8)

    upd_qkv = adam_update(w_qkv, moment_qkv, square_qkv, g_qkv, rate_matrix, weight_decay)
    upd_out = adam_update(w_out, moment_out, square_out, g_out, rate_matrix, weight_decay)
    upd_up = adam_update(w_up, moment_up, square_up, g_up, rate_matrix, weight_decay)
    upd_down = adam_update(w_down, moment_down, square_down, g_down, rate_matrix, weight_decay)
    upd_gains = adam_update(gains, moment_gains, square_gains, g_gain, rate_gain, 0.0)
    updates = (upd_qkv, upd_out, upd_up, upd_down, upd_gains)
    return (
        output.reshape(BLOCK, 1, D),
        input_grad.reshape(BLOCK, 1, D),
        *(u[0] for u in updates),
        *(u[1] for u in updates),
        *(u[2] for u in updates),
        *(u[0].astype(bf16) for u in updates),
    )


def solution(mesh):
    fine = Mesh(mesh.devices.reshape(2, 4, 2, 4, 2), ("zh", "x", "c", "y", "zl"))
    tokens_spec = P(SEQ, DP, None)
    rows_spec = P(None, DP + SEQ, None)
    gains_spec = P(None, None, DP + SEQ)
    masters = (rows_spec,) * 4 + (gains_spec,)
    return jax.shard_map(
        body,
        mesh=fine,
        in_specs=(tokens_spec, tokens_spec, P(DP, None)) + masters * 3,
        out_specs=(tokens_spec, tokens_spec) + masters * 4,
        check_vma=False,
    )
```

```python
import jax
import jax.numpy as jnp
from jax import lax
from jax.experimental import pallas as pl
from jax.experimental.pallas import tpu as pltpu
from jax.sharding import Mesh
from jax.sharding import PartitionSpec as P

D = 1024
HEADS = 16
HEAD_DIM = 64
FF = 4096
LAYERS = 2
STEP = 5
LENGTH = 1024
BLOCK = 128
QB = 256
GRANT = 48

norm_eps = 1e-05
beta_first = 0.9
beta_second = 0.95
adam_eps = 1e-08
weight_decay = 0.1
rate_matrix = 0.04
rate_gain = 0.4
masked_score = -1e30
score_scale = HEAD_DIM ** (-0.5)

bf16 = jnp.bfloat16
f32 = jnp.float32
SEQ = ("y", "zl")
DP = ("zh", "x", "c")
ZAX = ("zh", "zl")
XY = ("x", "y")
ALL = ("zh", "x", "c", "y", "zl")


def dot(a, b, dims):
    return lax.dot_general(a, b, (dims, ((), ())), preferred_element_type=f32)


def mm(a, b):
    return dot(a, b, ((1,), (0,)))


def mm_nt(a, b):
    return dot(a, b, ((1,), (1,)))


def mm_tn(a, b):
    return dot(a, b, ((0,), (0,)))


def swap_halves(x):
    lane = lax.broadcasted_iota(jnp.int32, x.shape, 1)
    return jnp.where((lane % 64) < 32, pltpu.roll(x, 96, 1), pltpu.roll(x, 32, 1))


def lane_mask(x, row):
    lane = lax.broadcasted_iota(jnp.int32, x.shape, 1)
    return jnp.where((lane // 64) == row, x, jnp.zeros_like(x))


def allowed_mask(start_row, keys, first_query):
    key = lax.broadcasted_iota(jnp.int32, (keys, QB), 0)
    query = lax.broadcasted_iota(jnp.int32, (keys, QB), 1) + first_query
    return (key >= start_row) & (key <= query)


def whole(count):
    return [pl.BlockSpec(memory_space=pltpu.VMEM)] * count


def rms_scale(values):
    return lax.rsqrt(jnp.mean(values * values, axis=-1, keepdims=True) + norm_eps)


def rms_norm(values, gain_row):
    return values * rms_scale(values) * gain_row


def rms_back(values, gain_row, grad):
    scale = rms_scale(values)
    unit = values * scale
    scaled = grad * gain_row
    inner = jnp.mean(scaled * unit, axis=-1, keepdims=True)
    return scale * (scaled - unit * inner), jnp.sum(grad * unit, axis=0, keepdims=True)


def adam_update(master, moment_one, moment_two, gradient, rate, decay):
    moment_new = beta_first * moment_one + (1.0 - beta_first) * gradient
    square_new = beta_second * moment_two + (1.0 - beta_second) * gradient * gradient
    moment_hat = moment_new / (1.0 - beta_first**STEP)
    square_hat = square_new / (1.0 - beta_second**STEP)
    updated = master - rate * (moment_hat / (jnp.sqrt(square_hat) + adam_eps) + decay * master)
    return (updated, moment_new, square_new)


def other_core(x):
    return lax.ppermute(x, "c", [(0, 1), (1, 0)])


def seq_swap(x):
    return lax.all_to_all(x, SEQ, 0, 0, tiled=True)


CUBE, PLANE, AXIS = 0, 3, 4
QKV, OUT, UP, DOWN, GAIN, QKV_ONE, OUT_ONE = "qkv", "out", "up", "down", "gain", "qkv1", "out1"
WIDTH = {QKV: 1536, OUT: 512, UP: 2048, DOWN: 2048, GAIN: 128, QKV_ONE: 1536, OUT_ONE: 512}
SHAPE = {QKV: (1024, 1536), OUT: (512, 1024), UP: (1024, 2048), DOWN: (2048, 1024), GAIN: (1024, 128)}


def place(i):
    return (i // 64) * 2 + i % 2, (i // 16) % 4, (i // 8) % 2, (i // 2) % 4


def device_at(z, x, c, y):
    return (((z // 2) * 4 + x) * 2 + c) * 8 + y * 2 + z % 2


def pairs(axis, phase):
    found = []
    for i in range(128):
        z, x, c, y = place(i)
        mask = 3 if (c if phase else 1 - c) else 1
        x, y, z = (x ^ mask, y, z) if axis == 0 else (x, y ^ mask, z) if axis == 1 else (x, y, z ^ mask)
        found.append((i, device_at(z, x, c, y)))
    return found


PAIRS = {(axis, phase): pairs(axis, phase) for axis in range(3) for phase in range(2)}


def pair_swap(x, axis, phase):
    return lax.ppermute(x, ALL, PAIRS[axis, phase])


def add_low(a, b):
    return (a.astype(f32) + b.astype(f32)).astype(bf16)


def cube_groups():
    found = {}
    for i in range(128):
        z, x, c, y = place(i)
        shift, mask = (0, 1) if c else (1, 3)
        rank = ((x >> shift) & 1) * 4 + ((y >> shift) & 1) * 2 + ((z >> shift) & 1)
        key = (c,) + tuple(min(v, v ^ mask) for v in (x, y, z))
        found.setdefault(key, [0] * 8)[rank] = i
    return list(found.values())


CUBES = cube_groups()


def cube_all_to_all(x):
    return lax.all_to_all(x, ALL, 0, 0, axis_index_groups=CUBES, tiled=True)


def cube_round(cur, k):
    return [pair_swap(cur[g], (g + k) % 3, 1) for g in range(3)]


def join(cur, got):
    return [jnp.concatenate([x, y], axis=0) for x, y in zip(cur, got)]


def scatter_round(keep, send, k):
    cur = [add_low(x, y) for x, y in zip(keep, cube_round(send, k))]
    half = cur[0].shape[0] // 2
    return [x[:half] for x in cur], [x[half:] for x in cur]


def together(*values):
    return lax.optimization_barrier(values)


def unit_tables(mine):
    my_z, my_x, core, my_y = mine
    first = jnp.where(core == 0, 3, 1)
    last = jnp.where(core == 0, 1, 3)
    shift = jnp.where(core == 0, 1, 0)
    p = jnp.arange(64, dtype=jnp.int32)
    rows = []
    for g in range(5):
        if g < 3:
            at = [my_x, my_y, my_z]
            for k in range(3):
                at[(g + k) % 3] = at[(g + k) % 3] ^ (((p >> (3 + k)) & 1) * last)
            for axis in range(3):
                differs = ((at[axis] >> shift) & 1) ^ ((p >> (2 - axis)) & 1)
                at[axis] = at[axis] ^ (differs * first)
            x, y, z = at
        else:
            x, y = (p >> 4, (p >> 2) & 3) if g == PLANE else (p >> 4, my_y ^ (((p >> 2) & 1) * last) ^ (((p >> 3) & 1) * first))
            z = my_z ^ ((p & 1) * last) ^ (((p >> 1) & 1) * first)
        zh, zl = z >> 1, z & 1
        rows += [
            (((zh * 4 + x) * 2 + zl) * 4 + y) * 16,
            ((zh * 4 + x) * 4 + y) * 16,
            zl * 512,
            (((zh * 4 + x) * 4 + y) * 2 + zl) * 32,
        ]
    return jnp.stack(rows).astype(jnp.int32)


def segments(names, bounds):
    pieces = []
    start = 0
    for name in names:
        for part in range(2 if name == DOWN else 1):
            width = 1024 if name == DOWN else WIDTH[name]
            pieces.append((name, start, width, 16 * part))
            start += width
    found = []
    for ranges in bounds:
        group = []
        at = 0
        for a, b in ranges:
            for name, first, width, extra in pieces:
                lo, hi = max(a, first), min(b, first + width)
                if lo < hi:
                    group.append((name, at + lo - a, lo - first, hi - lo, extra))
            at += b - a
        found.append(group)
    return found


def whole_slice(tab, ref, name, group, p, column, count, extra):
    if name in (OUT, OUT_ONE):
        row = pl.multiple_of(tab[4 * group + 1, p], 16)
        col = pl.multiple_of(tab[4 * group + 2, p] + column, 128)
        return ref.at[pl.ds(row, 16), pl.ds(col, count)]
    if name == DOWN:
        row = pl.multiple_of(tab[4 * group + 3, p] + extra, 16)
    else:
        row = pl.multiple_of(tab[4 * group, p], 16)
    return ref.at[pl.ds(row, 16), pl.ds(column, count)]


class Layout:
    def __init__(self, names, cuts, order, per):
        self.names, self.cuts, self.order, self.per = names, cuts, order, per
        self.plan = segments(names, cuts)
        self.shapes = [(64 // per, 16, self.width(g)) for g in range(len(cuts)) for _ in range(per)]

    def width(self, g):
        return sum(b - a for a, b in self.cuts[g])

    def move(self, names, tab, wholes, buffers, sem_of, store):
        def step(i, carry):
            for g, group in enumerate(self.plan):
                for part in range(self.per):
                    at_buffer = g * self.per + part
                    for name, at, column, count, extra in group:
                        if name not in names:
                            continue
                        piece = buffers[at_buffer].at[i, :, pl.ds(at, count)]
                        place_in = i + part * (64 // self.per)
                        own = whole_slice(tab, wholes[name], name, self.order + g, place_in, column, count, extra)
                        ends = (own, piece) if store else (piece, own)
                        pltpu.make_async_copy(*ends, sem_of(name, at_buffer)).start()
            return carry

        lax.fori_loop(0, 64 // self.per, step, 0)


FIRST = Layout((QKV, OUT, GAIN), (((0, 768),), ((768, 1536),), ((1536, 2176),)), CUBE, 2)
SECOND = Layout(
    (UP, DOWN, QKV, OUT),
    (((0, 1408), (4096, 4736)), ((1408, 2816), (4736, 5376)), ((2816, 4096), (5376, 6144))),
    CUBE,
    2,
)
FEED = Layout((UP, DOWN), (((0, 4096),),), PLANE, 1)
FEED_ONE = Layout((UP, DOWN), (((0, 4096),),), AXIS, 1)
TAIL = Layout((QKV, OUT, QKV_ONE, OUT_ONE), (((0, 1408),), ((1408, 2816),), ((2816, 4096),)), CUBE, 2)


def wait_all(ref, sem):
    pltpu.make_async_copy(ref, ref, sem).wait()


def shape_of(name):
    return pltpu.VMEM(SHAPE[name], bf16)


def merge(a, b):
    low = lax.broadcasted_iota(jnp.int32, a.shape, 1) < 64
    return jnp.where(low, a, pltpu.roll(b, 64, 1)), jnp.where(low, pltpu.roll(a, 64, 1), b)


def halves():
    near, far = slice(0, BLOCK), slice(BLOCK, 2 * BLOCK)
    return ((near, far), (far, near))


def total(part, got, mine, theirs):
    return part[mine, :].astype(f32) + got[theirs, :].astype(f32)


class Refs:
    pass


def kernel_call(kernel, name, tables, dense=(), loaded=(), buffers=(), outs=(), stored=(), packed=(), scratch=()):
    hbm = pl.BlockSpec(memory_space=pltpu.HBM)
    where = pl.BlockSpec(memory_space=pl.ANY)
    counts = [len(x) for x in (dense, loaded, buffers, outs, stored, packed, scratch, loaded, stored)]

    def run(tab, *refs):
        r = Refs()
        parts = []
        for count in counts:
            parts.append(refs[:count])
            refs = refs[count:]
        r.dense, loads, r.buffers, r.outs, saves, r.packed, r.scratch, r.loaded, r.stored = parts
        load_sems, save_sems = refs
        for n, source in enumerate(loads):
            pltpu.make_async_copy(source, r.loaded[n], load_sems.at[n]).start()

        def ready():
            for n, source in enumerate(loads):
                pltpu.make_async_copy(source, r.loaded[n], load_sems.at[n]).wait()

        def save(n):
            pltpu.make_async_copy(r.stored[n], saves[n], save_sems.at[n]).start()

        r.ready, r.save = ready, save
        kernel(tab, r)
        for n, target in enumerate(saves):
            pltpu.make_async_copy(r.stored[n], target, save_sems.at[n]).wait()

    out = pl.pallas_call(
        run,
        out_shape=(*outs, *stored, *packed),
        in_specs=[pl.BlockSpec(memory_space=pltpu.SMEM)] + whole(len(dense)) + [hbm] * len(loaded) + [where] * len(buffers),
        out_specs=(*whole(len(outs)), *[hbm] * len(stored), *[where] * len(packed)),
        scratch_shapes=[
            *scratch,
            *[pltpu.VMEM(x.shape, x.dtype) for x in loaded],
            *[pltpu.VMEM(x.shape, x.dtype) for x in stored],
            pltpu.SemaphoreType.DMA((max(len(loaded), 1),)),
            pltpu.SemaphoreType.DMA((max(len(stored), 1),)),
        ],
        compiler_params=pltpu.CompilerParams(vmem_limit_bytes=GRANT * 1024 * 1024),
        name=name,
    )(tables, *dense, *loaded, *buffers)
    return out


def array(shape, kind):
    return jax.ShapeDtypeStruct(shape, kind)


ROWS_F32 = array((2 * BLOCK, D), f32)
ROWS_LOW = array((2 * BLOCK, D), bf16)
ROWS_WIDE = array((2 * BLOCK, 2048), bf16)
GAIN_ROWS = array((8, D), f32)


def gain_rows_kernel(tables, buffers):
    def kernel(tab, r):
        gain, sem = r.scratch
        FIRST.move((GAIN,), tab, {GAIN: gain}, r.buffers, lambda n, b: sem, False)
        wait_all(gain, sem)
        r.outs[0][...] = jnp.transpose(gain[...].astype(f32))[:8]

    scratch = [shape_of(GAIN), pltpu.SemaphoreType.DMA]
    return kernel_call(kernel, "gain_rows", tables, buffers=buffers, outs=[array((8, D), f32)], scratch=scratch)[0]


def att_forward(qkv, turn):
    def kernel(tab, r):
        (qkv_ref,), (att_ref,), (rot_ref, lse_ref), (att_t,) = r.dense, r.outs, r.stored, r.scratch
        cos_ref, sin_ref, start_ref = r.loaded
        q = qkv_ref[:, :, 0:128].reshape(LENGTH, 128).astype(f32)
        k = qkv_ref[:, :, 128:256].reshape(LENGTH, 128).astype(f32)
        v = qkv_ref[:, :, 256:384].reshape(LENGTH, 128)
        r.ready()
        cosine = cos_ref[...]
        sine = sin_ref[...]
        q = q * cosine + swap_halves(q) * sine
        k = k * cosine + swap_halves(k) * sine
        rot_ref[:, 0:128] = q.astype(bf16)
        rot_ref[:, 128:256] = k.astype(bf16)
        rot_ref[:, 256:384] = v
        r.save(0)
        v_t = jnp.transpose(v.astype(f32)).astype(bf16)
        for row in range(2):
            k_row = lane_mask(k, row).astype(bf16)
            for step in range(LENGTH // QB):
                first = step * QB
                keys = first + QB
                q_blk = rot_ref[first : first + QB, 0:128]
                s = mm_nt(k_row[:keys], q_blk) * score_scale
                ok = allowed_mask(start_ref[row : row + 1, first : first + QB], keys, first)
                s = jnp.where(ok, s, masked_score)
                top = jnp.max(s, axis=0, keepdims=True)
                e = jnp.exp(s - top)
                total = jnp.sum(e, axis=0, keepdims=True)
                lse_ref[row : row + 1, first : first + QB] = top + jnp.log(total)
                p = (e * (1.0 / total)).astype(bf16)
                att_t[row * 64 : row * 64 + 64, first : first + QB] = mm(v_t[row * 64 : row * 64 + 64, :keys], p)
        r.save(1)
        att_ref[...] = jnp.transpose(att_t[...]).astype(bf16).reshape(8, BLOCK, 128)

    return kernel_call(
        kernel,
        "att_forward",
        jnp.zeros((1,), jnp.int32),
        dense=(qkv,),
        loaded=turn,
        outs=[array((8, BLOCK, 128), bf16)],
        stored=[array((LENGTH, 384), bf16), array((8, LENGTH), f32)],
        scratch=[pltpu.VMEM((128, LENGTH), f32)],
    )


def att_backward(datt, rot, lse, turn):
    def kernel(tab, r):
        (datt_ref,), (out_ref,), (dk_acc, dv_acc, dq_t) = r.dense, r.outs, r.scratch
        rot_ref, lse_ref, cos_ref, sin_ref, start_ref = r.loaded
        datt = datt_ref[...].reshape(LENGTH, 128)
        dk_acc[...] = jnp.zeros_like(dk_acc)
        dv_acc[...] = jnp.zeros_like(dv_acc)
        r.ready()
        cosine = cos_ref[...]
        sine = sin_ref[...]
        q = rot_ref[:, 0:128]
        k = rot_ref[:, 128:256]
        v = rot_ref[:, 256:384]
        k_t = jnp.transpose(k.astype(f32)).astype(bf16)
        for row in range(2):
            q_row = lane_mask(q, row)
            datt_row = lane_mask(datt, row)
            for step in range(LENGTH // QB):
                first = step * QB
                keys = first + QB
                q_blk = q_row[first : first + QB]
                datt_blk = datt_row[first : first + QB]
                s = mm_nt(k[:keys], q_blk) * score_scale
                ok = allowed_mask(start_ref[row : row + 1, first : first + QB], keys, first)
                p = jnp.where(ok, jnp.exp(s - lse_ref[row : row + 1, first : first + QB]), 0.0)
                dp = mm_nt(v[:keys], datt_blk)
                delta = jnp.sum(p * dp, axis=0, keepdims=True)
                ds = (p * (dp - delta)).astype(bf16)
                dq_t[row * 64 : row * 64 + 64, first : first + QB] = mm(k_t[row * 64 : row * 64 + 64, :keys], ds)
                dk_acc[0:keys, :] += mm(ds, q_blk)
                dv_acc[0:keys, :] += mm(p.astype(bf16), datt_blk)
        dq = jnp.transpose(dq_t[...]) * score_scale
        dk = dk_acc[...] * score_scale
        out_ref[:, :, 0:128] = (dq * cosine - swap_halves(dq) * sine).astype(bf16).reshape(8, BLOCK, 128)
        out_ref[:, :, 128:256] = (dk * cosine - swap_halves(dk) * sine).astype(bf16).reshape(8, BLOCK, 128)
        out_ref[:, :, 256:384] = dv_acc[...].astype(bf16).reshape(8, BLOCK, 128)

    return kernel_call(
        kernel,
        "att_backward",
        jnp.zeros((1,), jnp.int32),
        dense=(datt,),
        loaded=(rot, lse, *turn),
        outs=[array((8, BLOCK, 384), bf16)],
        scratch=[pltpu.VMEM((LENGTH, 128), f32), pltpu.VMEM((LENGTH, 128), f32), pltpu.VMEM((128, LENGTH), f32)],
    )[0]


def qkv_forward(l, tables, gains, hidden, previous, source):
    layout, buffers = source

    def kernel(tab, r):
        gain, *below = r.dense
        rows_in, normed = r.loaded[0], r.stored[0]
        weight, sem = r.scratch
        layout.move((QKV,), tab, {QKV: weight}, r.buffers, lambda n, b: sem, False)
        r.ready()
        for mine, theirs in halves():
            rows = rows_in[mine, :]
            if below:
                down = total(*below, mine, theirs)
                r.stored[2][mine, :] = down
                rows = rows + rms_norm(down, gain[4 * l - 1 : 4 * l, :])
                r.stored[1][mine, :] = rows
            normed[mine, :] = rms_norm(rows, gain[4 * l : 4 * l + 1, :]).astype(bf16)
        for n in range(len(r.stored)):
            r.save(n)
        wait_all(weight, sem)
        for pair in range(4):
            mixed = mm(normed[...], weight[:, pair * 384 : pair * 384 + 384])
            for t in range(3):
                first, second = merge(
                    mixed[:BLOCK, t * 128 : t * 128 + 128], mixed[BLOCK:, t * 128 : t * 128 + 128]
                )
                r.outs[0][2 * pair, :, t * 128 : t * 128 + 128] = first.astype(bf16)
                r.outs[0][2 * pair + 1, :, t * 128 : t * 128 + 128] = second.astype(bf16)

    return kernel_call(
        kernel,
        "qkv_forward",
        tables,
        dense=(gains, *previous),
        loaded=(hidden,),
        buffers=buffers,
        outs=[array((8, BLOCK, 384), bf16)],
        stored=[ROWS_LOW] + ([ROWS_F32, ROWS_F32] if previous else []),
        scratch=[shape_of(QKV), pltpu.SemaphoreType.DMA],
    )


def out_forward(tables, att, source):
    layout, buffers = source

    def kernel(tab, r):
        (att_in,), (part,), (rows,), (weight, sem) = r.dense, r.outs, r.stored, r.scratch
        layout.move((OUT,), tab, {OUT: weight}, r.buffers, lambda n, b: sem, False)
        for pair in range(4):
            near, far = merge(att_in[2 * pair].astype(f32), att_in[2 * pair + 1].astype(f32))
            rows[:BLOCK, pair * 128 : pair * 128 + 128] = near.astype(bf16)
            rows[BLOCK:, pair * 128 : pair * 128 + 128] = far.astype(bf16)
        r.save(0)
        wait_all(weight, sem)
        part[...] = mm(rows[...], weight[...]).astype(bf16)

    return kernel_call(
        kernel,
        "out_forward",
        tables,
        dense=(att,),
        buffers=buffers,
        outs=[ROWS_LOW],
        stored=[array((2 * BLOCK, 512), bf16)],
        scratch=[shape_of(OUT), pltpu.SemaphoreType.DMA],
    )


def mlp_forward(l, tables, gains, branch, hidden, source):
    layout, buffers = source

    def kernel(tab, r):
        gain, part, got = r.dense
        summed, middle, normed, active, slope = r.stored
        up, down, sems = r.scratch
        targets = {UP: up, DOWN: down}
        for n, name in enumerate((UP, DOWN)):
            layout.move((name,), tab, targets, r.buffers, lambda _, b: sems.at[n], False)
        r.ready()
        for mine, theirs in halves():
            values = total(part, got, mine, theirs)
            summed[mine, :] = values
            rows = r.loaded[0][mine, :] + rms_norm(values, gain[4 * l + 1 : 4 * l + 2, :])
            middle[mine, :] = rows
            normed[mine, :] = rms_norm(rows, gain[4 * l + 2 : 4 * l + 3, :]).astype(bf16)
        for n in range(3):
            r.save(n)
        wait_all(up, sems.at[0])
        for f in range(0, 2048, 256):
            u = mm(normed[...], up[:, f : f + 256])
            phi = 0.5 * (1.0 + lax.erf(u * (0.5**0.5)))
            active[:, f : f + 256] = (u * phi).astype(bf16)
            slope[:, f : f + 256] = (phi + u * (jnp.exp(-0.5 * u * u) * 0.3989422804014327)).astype(bf16)
        for n in range(3, 5):
            r.save(n)
        wait_all(down, sems.at[1])
        for n in range(0, 1024, 256):
            r.outs[0][:, n : n + 256] = mm(active[...], down[:, n : n + 256]).astype(bf16)

    return kernel_call(
        kernel,
        "mlp_forward",
        tables,
        dense=(gains, *branch),
        loaded=(hidden,),
        buffers=buffers,
        outs=[ROWS_LOW],
        stored=[ROWS_F32, ROWS_F32, ROWS_LOW, ROWS_WIDE, ROWS_WIDE],
        scratch=[shape_of(UP), shape_of(DOWN), pltpu.SemaphoreType.DMA((2,))],
    )


def mlp_backward(l, tables, gains, grad_rows, above, down, kept, source, gain_grads):
    layout, buffers = source
    parts = len(down) == 2
    target = FEED_ONE if l == 1 else FEED

    def kernel(tab, r):
        gain, gain_rows, *near = r.dense
        grad_in, active, slope, before, *rest = r.loaded
        up, down_weight, grad_up, grad_down, d_up, rows, sems = r.scratch
        (packed,) = r.packed
        weights = {UP: up, DOWN: down_weight}
        for n, name in enumerate((DOWN, UP)):
            layout.move((name,), tab, weights, r.buffers, lambda _, b: sems.at[n], False)
        wholes = {UP: grad_up, DOWN: grad_down}
        r.ready()
        r.outs[1][...] = gain_rows[...]
        for mine, theirs in halves():
            grad = grad_in[mine, :]
            if above:
                back, gain_four = rms_back(rest[0][mine, :], gain[4 * l + 4 : 4 * l + 5, :], total(*near, mine, theirs))
                grad = grad + back
                r.outs[2][mine, :] = grad
            values = total(*near, mine, theirs) if parts else rest[1][mine, :]
            back, gain_row = rms_back(values, gain[4 * l + 3 : 4 * l + 4, :], grad)
            rows[mine, :] = back.astype(bf16)
            if mine.start == 0:
                r.outs[1][4 * l + 3 : 4 * l + 4, :] = gain_row
                if above:
                    r.outs[1][4 * l + 4 : 4 * l + 5, :] = gain_four
        for f in range(0, 2048, 512):
            grad_down[f : f + 512, :] = mm_tn(active[:, f : f + 512], rows[...]).astype(bf16)
        target.move((DOWN,), tab, wholes, [packed], lambda _, b: sems.at[2], True)
        wait_all(down_weight, sems.at[0])
        for f in range(0, 2048, 512):
            d_active = mm_nt(rows[...], down_weight[f : f + 512, :])
            d_up[:, f : f + 512] = (d_active * slope[:, f : f + 512].astype(f32)).astype(bf16)
            grad_up[:, f : f + 512] = mm_tn(before[...], d_up[:, f : f + 512]).astype(bf16)
        target.move((UP,), tab, wholes, [packed], lambda _, b: sems.at[2], True)
        wait_all(up, sems.at[1])
        for n in range(0, 1024, 256):
            r.outs[0][:, n : n + 256] = mm_nt(d_up[...], up[n : n + 256, :]).astype(bf16)
        wait_all(packed, sems.at[2])

    *outs, packed = kernel_call(
        kernel,
        "mlp_backward",
        tables,
        dense=(gains, gain_grads, *(down if parts else above[:2])),
        loaded=(grad_rows, *kept, *((above[2], down[0]) if above else ())),
        buffers=buffers,
        outs=[ROWS_LOW, GAIN_ROWS] + ([ROWS_F32] if above else []),
        packed=[array(target.shapes[0], bf16)],
        scratch=[
            shape_of(UP),
            shape_of(DOWN),
            shape_of(UP),
            shape_of(DOWN),
            pltpu.VMEM((2 * BLOCK, 2048), bf16),
            pltpu.VMEM((2 * BLOCK, D), bf16),
            pltpu.SemaphoreType.DMA((3,)),
        ],
    )
    return packed, *outs


def out_backward(l, tables, gains, d_norm, grad_rows, kept, source, gain_grads):
    layout, buffers = source

    def kernel(tab, r):
        gain, gain_rows, d_part, d_got, *rest = r.dense
        middle, summed, att_rows, *more = r.loaded
        d_att, gain_out = r.outs
        d_middle, grad = r.stored
        weight, rows, sem = r.scratch
        grad_in = (rest + more)[0]
        layout.move((OUT,), tab, {OUT: weight}, r.buffers, lambda n, b: sem, False)
        gain_out[...] = gain_rows[...]
        r.ready()
        for mine, theirs in halves():
            back, row_two = rms_back(middle[mine, :], gain[4 * l + 2 : 4 * l + 3, :], total(d_part, d_got, mine, theirs))
            back = grad_in[mine, :] + back
            d_middle[mine, :] = back
            back, row_one = rms_back(summed[mine, :], gain[4 * l + 1 : 4 * l + 2, :], back)
            rows[mine, :] = back.astype(bf16)
            if mine.start == 0:
                gain_out[4 * l + 1 : 4 * l + 2, :] = row_one
                gain_out[4 * l + 2 : 4 * l + 3, :] = row_two
        r.save(0)
        wait_all(weight, sem)
        for pair in range(4):
            back = mm_nt(rows[...], weight[pair * 128 : pair * 128 + 128, :])
            first, second = merge(back[:BLOCK], back[BLOCK:])
            d_att[2 * pair] = first.astype(bf16)
            d_att[2 * pair + 1] = second.astype(bf16)
        grad[...] = mm_tn(att_rows[...], rows[...]).astype(bf16)
        r.save(1)

    near = l == 0
    return kernel_call(
        kernel,
        "out_backward",
        tables,
        dense=(gains, gain_grads, *d_norm) + ((grad_rows,) if near else ()),
        loaded=(*kept,) + (() if near else (grad_rows,)),
        buffers=buffers,
        outs=[array((8, BLOCK, 128), bf16), GAIN_ROWS],
        stored=[ROWS_F32, array(SHAPE[OUT], bf16)],
        scratch=[shape_of(OUT), pltpu.VMEM((2 * BLOCK, D), bf16), pltpu.SemaphoreType.DMA],
    )


def last_norm(gains, d_norm, grad_rows, hidden, gain_grads):
    def kernel(tab, r):
        gain, gain_rows, d_part, d_got = r.dense
        grad_in, entered = r.loaded
        r.ready()
        mine, theirs = halves()[0]
        back, row = rms_back(entered[mine, :], gain[0:1, :], total(d_part, d_got, mine, theirs))
        r.outs[0][...] = (grad_in[mine, :] + back).astype(bf16)
        r.outs[1][...] = gain_rows[...]
        r.outs[1][0:1, :] = row

    return kernel_call(
        kernel,
        "last_norm",
        jnp.zeros((1,), jnp.int32),
        dense=(gains, gain_grads, *d_norm),
        loaded=(grad_rows, hidden),
        outs=[array((BLOCK, D), bf16), GAIN_ROWS],
    )


def qkv_backward(l, tables, d_mixed, normed, source, held):
    layout, buffers = source
    pack = l == 0

    def kernel(tab, r):
        (d_in,), before = r.dense, r.loaded[0]
        weight, d_rows, sems, *grad = r.scratch
        grad = grad[0] if pack else r.stored[0]
        layout.move((QKV,), tab, {QKV: weight}, r.buffers, lambda n, b: sems.at[0], False)
        for pair in range(4):
            for t in range(3):
                a, b = merge(
                    d_in[2 * pair, :, t * 128 : t * 128 + 128].astype(f32),
                    d_in[2 * pair + 1, :, t * 128 : t * 128 + 128].astype(f32),
                )
                at = pair * 384 + t * 128
                d_rows[:BLOCK, at : at + 128] = a.astype(bf16)
                d_rows[BLOCK:, at : at + 128] = b.astype(bf16)
        r.ready()
        for f in range(0, 1536, 384):
            grad[:, f : f + 384] = mm_tn(before[...], d_rows[:, f : f + 384]).astype(bf16)
        if pack:
            wholes = {QKV: grad, OUT: r.loaded[1], QKV_ONE: r.loaded[2], OUT_ONE: r.loaded[3]}
            TAIL.move(TAIL.names, tab, wholes, r.packed, lambda n, b: sems.at[1 + b], True)
        else:
            r.save(0)
        wait_all(weight, sems.at[0])
        for n in range(0, 1024, 256):
            r.outs[0][:, n : n + 256] = mm_nt(d_rows[...], weight[n : n + 256, :]).astype(bf16)
        for n, target in enumerate(r.packed):
            wait_all(target, sems.at[1 + n])

    return kernel_call(
        kernel,
        "qkv_backward",
        tables,
        dense=(d_mixed,),
        loaded=(normed, *held),
        buffers=buffers,
        outs=[ROWS_LOW],
        stored=[] if pack else [array(SHAPE[QKV], bf16)],
        packed=[array(shape, bf16) for shape in TAIL.shapes] if pack else [],
        scratch=[shape_of(QKV), pltpu.VMEM((2 * BLOCK, 1536), bf16), pltpu.SemaphoreType.DMA((7,))]
        + ([shape_of(QKV)] if pack else []),
    )


def fold(cur, axis, phase):
    half = cur.shape[0] // 2
    return add_low(cur[:half], pair_swap(cur[half:], axis, phase))


CROSS = {
    flip: [
        (device_at(z, x, c, y), device_at((z // 2) * 2 + c, x, (z % 2) ^ flip, y))
        for z in range(4)
        for x in range(4)
        for c in range(2)
        for y in range(4)
    ]
    for flip in range(2)
}
CROSS_BACK = {flip: [(b, a) for a, b in CROSS[flip]] for flip in range(2)}


def rows_to_units(halves, zl, core):
    near = lax.ppermute(jnp.where(zl == 0, halves[0], halves[1]), ALL, CROSS[0])
    far = lax.ppermute(jnp.where(zl == 0, halves[1], halves[0]), ALL, CROSS[1])
    return jnp.where(core == 0, jnp.concatenate([near, far], axis=0), jnp.concatenate([far, near], axis=0))


def units_to_rows(units, zl, core):
    near = lax.ppermute(jnp.where(core == 0, units[:8], units[8:]), ALL, CROSS_BACK[0])
    far = lax.ppermute(jnp.where(core == 0, units[8:], units[:8]), ALL, CROSS_BACK[1])
    return jnp.where(zl == 0, jnp.stack([near, far]), jnp.stack([far, near]))


def zl_swap(x):
    return lax.ppermute(x, "zl", [(0, 1), (1, 0)])


def out_to_unit(out, zl):
    low, high = out[..., :512], out[..., 512:]
    kept = jnp.where(zl == 0, low, high)
    got = zl_swap(jnp.where(zl == 0, high, low))
    return jnp.where(zl == 0, jnp.concatenate([kept, got], axis=1), jnp.concatenate([got, kept], axis=1))


def out_to_rows(units, zl):
    top, bottom = units[:, :8], units[:, 8:]
    kept = jnp.where(zl == 0, top, bottom)
    got = zl_swap(jnp.where(zl == 0, bottom, top))
    return jnp.where(zl == 0, jnp.concatenate([kept, got], axis=-1), jnp.concatenate([got, kept], axis=-1))


def body(
    tokens,
    cotangent,
    lengths,
    w_qkv,
    w_out,
    w_up,
    w_down,
    gains,
    moment_qkv,
    moment_out,
    moment_up,
    moment_down,
    moment_gains,
    square_qkv,
    square_out,
    square_up,
    square_down,
    square_gains,
):
    core = lax.axis_index("c")
    zl = lax.axis_index("zl")
    my_z = lax.axis_index("zh") * 2 + zl
    tables = unit_tables((my_z, lax.axis_index("x"), core, lax.axis_index("y")))

    both = jnp.concatenate([lengths, other_core(lengths)], axis=0)
    ends = jnp.cumsum(both, axis=-1)
    starts = ends - both
    places = jnp.arange(LENGTH, dtype=jnp.int32)
    doc_ids = jnp.sum((places[None, :, None] >= ends[:, None, :]).astype(jnp.int32), axis=-1)
    picked = doc_ids[:, :, None] == jnp.arange(4, dtype=jnp.int32)[None, None, :]
    first_place = jnp.sum(jnp.where(picked, starts[:, None, :], 0), axis=-1)
    positions = (places[None, :] - first_place).astype(f32)
    inverse = 10000.0 ** (-jnp.arange(32, dtype=f32) / 32)
    angle = positions[:, :, None] * inverse
    cos_half = jnp.cos(angle)
    sin_half = jnp.sin(angle)
    cosine = jnp.concatenate([cos_half[0], cos_half[0], cos_half[1], cos_half[1]], axis=-1)
    sine = jnp.concatenate([-sin_half[0], sin_half[0], -sin_half[1], sin_half[1]], axis=-1)
    start_rows = jnp.concatenate([first_place, jnp.zeros((6, LENGTH), jnp.int32)], axis=0)

    qkv_halves = w_qkv.astype(bf16).reshape(LAYERS, 8, 3, 4, 2, 2, 64)
    qkv_halves = qkv_halves.transpose(5, 1, 0, 3, 2, 4, 6).reshape(2, 8, LAYERS * 1536)
    up_halves = w_up.astype(bf16).reshape(LAYERS, 8, 8, 2, 256).transpose(3, 1, 0, 2, 4).reshape(2, 8, LAYERS * 2048)
    gain_rows = gains.astype(bf16).reshape(8, 8).T
    gain_rows = jnp.broadcast_to(jnp.pad(gain_rows, ((0, 0), (0, 120)))[None], (2, 8, 128))
    units = rows_to_units(jnp.concatenate([qkv_halves, up_halves, gain_rows], axis=-1), zl, core)
    qkv_units, up_units, gain_unit = units[:, :3072], units[:, 3072:7168], units[:, 7168:]
    out_units = out_to_unit(w_out.astype(bf16), zl)
    down_units = w_down.astype(bf16).reshape(LAYERS, 2, 16, 1024).transpose(0, 2, 1, 3).reshape(LAYERS, 16, 2048)
    start_space = jnp.concatenate(
        [
            qkv_units[:, :1536],
            out_units[0],
            gain_unit,
            up_units[:, :2048],
            down_units[0],
            qkv_units[:, 1536:],
            out_units[1],
        ],
        axis=-1,
    )
    token_rows = tokens.reshape(BLOCK, D)
    hidden = jnp.concatenate([token_rows, other_core(token_rows)], axis=0).astype(f32)
    start_space, cosine, sine, start_rows, tables, hidden = together(
        start_space, cosine, sine, start_rows, tables, hidden
    )
    line = jnp.concatenate([up_units[:, 2048:], down_units[1]], axis=-1)[None]
    line_got = pair_swap(line, 2, 1)
    eight = cube_all_to_all(jnp.broadcast_to(start_space[None], (8,) + start_space.shape))
    line, line_got, eight = together(line, line_got, eight)
    line = jnp.concatenate([line, line_got], axis=0)
    cur = [
        jnp.concatenate([eight[..., a:b] for a, b in FIRST.cuts[g]] + [eight[..., 2176 + a : 2176 + b] for a, b in SECOND.cuts[g]], axis=-1)
        for g in range(3)
    ]
    line, line_got, got = together(line, pair_swap(line, 2, 0), cube_round(cur, 0))
    line = jnp.concatenate([line, line_got], axis=0)
    cur = join(cur, got)
    got = cube_round(cur, 1)
    sizes = [FIRST.width(g) for g in range(3)]
    first = join([x[..., :n] for x, n in zip(cur, sizes)], [x[..., :n] for x, n in zip(got, sizes)])
    second = join([x[..., n:] for x, n in zip(cur, sizes)], [x[..., n:] for x, n in zip(got, sizes)])
    first_got = cube_round(first, 2)
    first_got, second = together(first_got, second)
    second_got = cube_round(second, 2)
    first_buffers = [buffer for pair in zip(first, first_got) for buffer in pair]
    gains_used = gain_rows_kernel(tables, first_buffers)

    mixed, normed = qkv_forward(0, tables, gains_used, hidden, (), (FIRST, first_buffers))
    mixed, line, second_got = together(mixed, line, second_got)
    feed_buffer = lax.all_gather(line, XY, axis=0, tiled=True)
    second_buffers = [buffer for pair in zip(second, second_got) for buffer in pair]
    attn_source = (FIRST, first_buffers), (SECOND, second_buffers)
    feed_source = (SECOND, second_buffers), (FEED, [feed_buffer])

    turn = cosine, sine, start_rows
    previous = ()
    kept = []
    for l in range(LAYERS):
        if previous:
            mixed, normed, hidden, down_sum = qkv_forward(l, tables, gains_used, hidden, previous, attn_source[l])
        att_mine, rot, lse = att_forward(seq_swap(mixed), turn)
        branch, att = out_forward(tables, seq_swap(att_mine), attn_source[l])
        branch = branch, other_core(branch)
        down, branch_sum, middle, normed_mlp, active, slope = mlp_forward(
            l, tables, gains_used, branch, hidden, feed_source[l]
        )
        down = down, other_core(down)
        kept.append((hidden, normed, rot, lse, (middle, branch_sum, att), (active, slope, normed_mlp)))
        previous, hidden = down, middle
    hidden = middle[:BLOCK] + rms_norm(down[0][:BLOCK].astype(f32) + down[1][BLOCK:].astype(f32), gains_used[7:8])
    output = hidden.astype(bf16)

    grad_rows = cotangent.reshape(BLOCK, D)
    grad_rows = jnp.concatenate([grad_rows, other_core(grad_rows)], axis=0).astype(f32)
    gain_grads = jnp.zeros((8, D), f32)
    held = ()
    scattered = [None] * LAYERS
    above = ()
    for l in reversed(range(LAYERS)):
        hidden, normed, rot, lse, kept_out, kept_mlp = kept[l]
        packed, d_norm, gain_grads, *rest = mlp_backward(
            l, tables, gains_used, grad_rows, above, down, kept_mlp, feed_source[l], gain_grads
        )
        if above:
            (grad_rows,) = rest
        packed, d_norm = together(packed, d_norm)
        scattered[l] = lax.psum_scatter(
            packed.reshape(1024, -1), "x" if l == 1 else XY, scatter_dimension=0, tiled=True
        ).reshape(-1, 16, 4096)
        d_norm = d_norm, other_core(d_norm)
        d_att, gain_grads, d_middle, grad_wout = out_backward(
            l, tables, gains_used, d_norm, grad_rows, kept_out, attn_source[l], gain_grads
        )
        d_mixed = seq_swap(att_backward(seq_swap(d_att), rot, lse, turn))
        d_norm, *held = qkv_backward(l, tables, d_mixed, normed, attn_source[l], (grad_wout, *held) if l == 0 else ())
        d_norm = d_norm, other_core(d_norm)
        if l == 1:
            held = held[0], grad_wout
        grad_rows = d_middle
        above = (*d_norm, hidden)
        down = (down_sum,)
    input_grad, gain_grads = last_norm(gains_used, d_norm, grad_rows, hidden, gain_grads)

    tail = [held[0], held[2], held[4]], [held[1], held[3], held[5]]
    tail = scatter_round(*tail, 2)
    feed_zero, feed_one = scattered
    feed_one = fold(feed_one, 1, 0)

    gain_sum = gain_grads.reshape(8, 128, 8).transpose(1, 0, 2).reshape(128, 1, 64)
    gain_sum = lax.all_to_all(gain_sum, ALL, 0, 0, tiled=True)
    tail, feed_one, gain_sum = together(tail, feed_one, gain_sum)
    g_gain = jnp.sum(gain_sum, axis=0).reshape(LAYERS, 4, 8)

    tail = scatter_round(*tail, 1)
    feed_one = fold(feed_one, 1, 1)
    feed_zero = fold(feed_zero, 2, 0)
    tail, feed_zero, feed_one = together(tail, feed_zero, feed_one)
    tail = scatter_round(*tail, 0)
    feed_one = fold(feed_one, 2, 0)
    feed_zero = fold(feed_zero, 2, 1)[0]
    tail, feed_zero, feed_one = together(tail, feed_zero, feed_one)
    feed_one = fold(feed_one, 2, 1)[0]
    tail_own = jnp.concatenate([jnp.concatenate(x, axis=-1) for x in tail], axis=0)
    tail_own = jnp.sum(cube_all_to_all(tail_own).astype(f32), axis=0).astype(bf16)

    g_out_units = jnp.stack([tail_own[:, 1536:2048], tail_own[:, 3584:]])
    g_down = jnp.stack([feed_zero[:, 2048:], feed_one[:, 2048:]])
    g_down = g_down.reshape(LAYERS, 16, 2, 1024).transpose(0, 2, 1, 3).reshape(LAYERS, 32, 1024).astype(f32)
    both = jnp.concatenate(
        [tail_own[:, :1536], tail_own[:, 2048:3584], feed_zero[:, :2048], feed_one[:, :2048]], axis=-1
    )
    both, g_out_units = together(both, g_out_units)
    g_out = out_to_rows(g_out_units, zl).astype(f32)
    both = units_to_rows(both, zl, core).astype(f32)
    g_qkv = both[..., :3072].reshape(2, 8, LAYERS, 4, 3, 2, 64).transpose(2, 1, 4, 3, 5, 0, 6).reshape(LAYERS, 8, 3 * D)
    g_up = both[..., 3072:].reshape(2, 8, LAYERS, 8, 256).transpose(2, 1, 3, 0, 4).reshape(LAYERS, 8, FF)

    upd_qkv = adam_update(w_qkv, moment_qkv, square_qkv, g_qkv, rate_matrix, weight_decay)
    upd_out = adam_update(w_out, moment_out, square_out, g_out, rate_matrix, weight_decay)
    upd_up = adam_update(w_up, moment_up, square_up, g_up, rate_matrix, weight_decay)
    upd_down = adam_update(w_down, moment_down, square_down, g_down, rate_matrix, weight_decay)
    upd_gains = adam_update(gains, moment_gains, square_gains, g_gain, rate_gain, 0.0)
    updates = (upd_qkv, upd_out, upd_up, upd_down, upd_gains)
    return (
        output.reshape(BLOCK, 1, D),
        input_grad.reshape(BLOCK, 1, D),
        *(u[0] for u in updates),
        *(u[1] for u in updates),
        *(u[2] for u in updates),
        *(u[0].astype(bf16) for u in updates),
    )


def solution(mesh):
    fine = Mesh(mesh.devices.reshape(2, 4, 2, 4, 2), ("zh", "x", "c", "y", "zl"))
    tokens_spec = P(SEQ, DP, None)
    rows_spec = P(None, DP + SEQ, None)
    gains_spec = P(None, None, DP + SEQ)
    masters = (rows_spec,) * 4 + (gains_spec,)
    return jax.shard_map(
        body,
        mesh=fine,
        in_specs=(tokens_spec, tokens_spec, P(DP, None)) + masters * 3,
        out_specs=(tokens_spec, tokens_spec) + masters * 4,
        check_vma=False,
    )
```

```python
import jax
import jax.numpy as jnp
from jax import lax
from jax.experimental import pallas as pl
from jax.experimental.pallas import tpu as pltpu
from jax.sharding import Mesh
from jax.sharding import PartitionSpec as P

D = 1024
HEADS = 16
HEAD_DIM = 64
FF = 4096
LAYERS = 2
STEP = 5
LENGTH = 1024
BLOCK = 128
QB = 256
GRANT = 48

norm_eps = 1e-05
beta_first = 0.9
beta_second = 0.95
adam_eps = 1e-08
weight_decay = 0.1
rate_matrix = 0.04
rate_gain = 0.4
masked_score = -1e30
score_scale = HEAD_DIM ** (-0.5)

bf16 = jnp.bfloat16
f32 = jnp.float32
SEQ = ("y", "zl")
DP = ("zh", "x", "c")
ZAX = ("zh", "zl")
XY = ("x", "y")
ALL = ("zh", "x", "c", "y", "zl")


def dot(a, b, dims):
    return lax.dot_general(a, b, (dims, ((), ())), preferred_element_type=f32)


def mm(a, b):
    return dot(a, b, ((1,), (0,)))


def mm_nt(a, b):
    return dot(a, b, ((1,), (1,)))


def mm_tn(a, b):
    return dot(a, b, ((0,), (0,)))


def swap_halves(x):
    lane = lax.broadcasted_iota(jnp.int32, x.shape, 1)
    return jnp.where((lane % 64) < 32, pltpu.roll(x, 96, 1), pltpu.roll(x, 32, 1))


def lane_mask(x, row):
    lane = lax.broadcasted_iota(jnp.int32, x.shape, 1)
    return jnp.where((lane // 64) == row, x, jnp.zeros_like(x))


def allowed_mask(start_row, keys, first_query):
    key = lax.broadcasted_iota(jnp.int32, (keys, QB), 0)
    query = lax.broadcasted_iota(jnp.int32, (keys, QB), 1) + first_query
    return (key >= start_row) & (key <= query)


def whole(count):
    return [pl.BlockSpec(memory_space=pltpu.VMEM)] * count


def rms_scale(values):
    return lax.rsqrt(jnp.mean(values * values, axis=-1, keepdims=True) + norm_eps)


def rms_norm(values, gain_row):
    return values * rms_scale(values) * gain_row


def rms_back(values, gain_row, grad):
    scale = rms_scale(values)
    unit = values * scale
    scaled = grad * gain_row
    inner = jnp.mean(scaled * unit, axis=-1, keepdims=True)
    return scale * (scaled - unit * inner), jnp.sum(grad * unit, axis=0, keepdims=True)


def adam_update(master, moment_one, moment_two, gradient, rate, decay):
    moment_new = beta_first * moment_one + (1.0 - beta_first) * gradient
    square_new = beta_second * moment_two + (1.0 - beta_second) * gradient * gradient
    moment_hat = moment_new / (1.0 - beta_first**STEP)
    square_hat = square_new / (1.0 - beta_second**STEP)
    updated = master - rate * (moment_hat / (jnp.sqrt(square_hat) + adam_eps) + decay * master)
    return (updated, moment_new, square_new)


def other_core(x):
    return lax.ppermute(x, "c", [(0, 1), (1, 0)])


def seq_swap(x):
    return lax.all_to_all(x, SEQ, 0, 0, tiled=True)


CUBE, PLANE, AXIS = (0, 1, 2), (3,), (4,)
QKV, OUT, UP, DOWN, GAIN, QKV_ONE, OUT_ONE = "qkv", "out", "up", "down", "gain", "qkv1", "out1"
WIDTH = {QKV: 1536, OUT: 512, UP: 2048, DOWN: 2048, GAIN: 128, QKV_ONE: 1536, OUT_ONE: 512}
SHAPE = {QKV: (1024, 1536), OUT: (512, 1024), UP: (1024, 2048), DOWN: (2048, 1024), GAIN: (1024, 128)}


def place(i):
    return (i // 64) * 2 + i % 2, (i // 16) % 4, (i // 8) % 2, (i // 2) % 4


def device_at(z, x, c, y):
    return (((z // 2) * 4 + x) * 2 + c) * 8 + y * 2 + z % 2


def pairs(axis, phase):
    found = []
    for i in range(128):
        z, x, c, y = place(i)
        mask = 3 if (c if phase else 1 - c) else 1
        x, y, z = (x ^ mask, y, z) if axis == 0 else (x, y ^ mask, z) if axis == 1 else (x, y, z ^ mask)
        found.append((i, device_at(z, x, c, y)))
    return found


PAIRS = {(axis, phase): pairs(axis, phase) for axis in range(3) for phase in range(2)}


def pair_swap(x, axis, phase):
    return lax.ppermute(x, ALL, PAIRS[axis, phase])


def add_low(a, b):
    return (a.astype(f32) + b.astype(f32)).astype(bf16)


def cube_groups():
    found = {}
    for i in range(128):
        z, x, c, y = place(i)
        shift, mask = (0, 1) if c else (1, 3)
        rank = ((x >> shift) & 1) * 4 + ((y >> shift) & 1) * 2 + ((z >> shift) & 1)
        key = (c,) + tuple(min(v, v ^ mask) for v in (x, y, z))
        found.setdefault(key, [0] * 8)[rank] = i
    return list(found.values())


CUBES = cube_groups()


def cube_all_to_all(x):
    return lax.all_to_all(x, ALL, 0, 0, axis_index_groups=CUBES, tiled=True)


AXES = {0: (0, 1, 2), 1: (1, 2, 0), 2: (2, 0, 1), 5: (0, 2, 1)}


def cube_round(cur, k, orders=(0, 1, 2)):
    return [pair_swap(x, AXES[g][k], 1) for x, g in zip(cur, orders)]


def join(cur, got):
    return [jnp.concatenate([x, y], axis=0) for x, y in zip(cur, got)]


def scatter_round(keep, send, k):
    got = cube_round(send, k, (0, 5))
    half = keep[0].shape[0] // 2
    send = [add_low(x[half:], y[half:]) for x, y in zip(keep, got)]
    return [add_low(x[:half], y[:half]) for x, y in zip(keep, got)], send


def together(*values):
    return lax.optimization_barrier(values)


def unit_tables(mine):
    my_z, my_x, core, my_y = mine
    first = jnp.where(core == 0, 3, 1)
    last = jnp.where(core == 0, 1, 3)
    shift = jnp.where(core == 0, 1, 0)
    p = jnp.arange(64, dtype=jnp.int32)
    rows = []
    for g in range(6):
        if g in AXES:
            at = [my_x, my_y, my_z]
            for k, axis in enumerate(AXES[g]):
                at[axis] = at[axis] ^ (((p >> (3 + k)) & 1) * last)
            for axis in range(3):
                differs = ((at[axis] >> shift) & 1) ^ ((p >> (2 - axis)) & 1)
                at[axis] = at[axis] ^ (differs * first)
            x, y, z = at
        else:
            x, y = (p >> 4, (p >> 2) & 3) if g == 3 else (p >> 4, my_y ^ (((p >> 2) & 1) * last) ^ (((p >> 3) & 1) * first))
            z = my_z ^ ((p & 1) * last) ^ (((p >> 1) & 1) * first)
        zh, zl = z >> 1, z & 1
        rows += [
            (((zh * 4 + x) * 2 + zl) * 4 + y) * 16,
            ((zh * 4 + x) * 4 + y) * 16,
            zl * 512,
            (((zh * 4 + x) * 4 + y) * 2 + zl) * 32,
        ]
    return jnp.stack(rows).astype(jnp.int32)


def segments(names, bounds):
    pieces = []
    start = 0
    for name in names:
        for part in range(2 if name == DOWN else 1):
            width = 1024 if name == DOWN else WIDTH[name]
            pieces.append((name, start, width, 16 * part))
            start += width
    found = []
    for ranges in bounds:
        group = []
        at = 0
        for a, b in ranges:
            for name, first, width, extra in pieces:
                lo, hi = max(a, first), min(b, first + width)
                if lo < hi:
                    group.append((name, at + lo - a, lo - first, hi - lo, extra))
            at += b - a
        found.append(group)
    return found


def whole_slice(tab, ref, name, group, p, column, count, extra):
    if name in (OUT, OUT_ONE):
        row = pl.multiple_of(tab[4 * group + 1, p], 16)
        col = pl.multiple_of(tab[4 * group + 2, p] + column, 128)
        return ref.at[pl.ds(row, 16), pl.ds(col, count)]
    if name == DOWN:
        row = pl.multiple_of(tab[4 * group + 3, p] + extra, 16)
    else:
        row = pl.multiple_of(tab[4 * group, p], 16)
    return ref.at[pl.ds(row, 16), pl.ds(column, count)]


class Layout:
    def __init__(self, names, cuts, order, per):
        self.names, self.cuts, self.order, self.per = names, cuts, order, per
        self.plan = segments(names, cuts)
        self.shapes = [(64 // per, 16, self.width(g)) for g in range(len(cuts)) for _ in range(per)]

    def width(self, g):
        return sum(b - a for a, b in self.cuts[g])

    def move(self, names, tab, wholes, buffers, sem_of, store):
        def step(i, carry):
            for g, group in enumerate(self.plan):
                for part in range(self.per):
                    at_buffer = g * self.per + part
                    for name, at, column, count, extra in group:
                        if name not in names:
                            continue
                        piece = buffers[at_buffer].at[i, :, pl.ds(at, count)]
                        place_in = i + part * (64 // self.per)
                        own = whole_slice(tab, wholes[name], name, self.order[g], place_in, column, count, extra)
                        ends = (own, piece) if store else (piece, own)
                        pltpu.make_async_copy(*ends, sem_of(name, at_buffer)).start()
            return carry

        lax.fori_loop(0, 64 // self.per, step, 0)


FIRST = Layout((QKV, OUT, GAIN), (((0, 768),), ((768, 1536),), ((1536, 2176),)), CUBE, 2)
SECOND = Layout(
    (UP, DOWN, QKV, OUT),
    (((0, 1408), (4096, 4736)), ((1408, 2816), (4736, 5376)), ((2816, 4096), (5376, 6144))),
    CUBE,
    2,
)
FEED = Layout((UP, DOWN), (((0, 4096),),), PLANE, 1)
FEED_SUM = Layout((UP, DOWN), (((0, 4096),),), AXIS, 1)
TAIL = Layout((QKV, OUT, QKV_ONE, OUT_ONE), (((0, 2048),), ((2048, 4096),)), (0, 5), 2)


def wait_all(ref, sem):
    pltpu.make_async_copy(ref, ref, sem).wait()


def shape_of(name):
    return pltpu.VMEM(SHAPE[name], bf16)


def merge(a, b):
    low = lax.broadcasted_iota(jnp.int32, a.shape, 1) < 64
    return jnp.where(low, a, pltpu.roll(b, 64, 1)), jnp.where(low, pltpu.roll(a, 64, 1), b)


def halves():
    near, far = slice(0, BLOCK), slice(BLOCK, 2 * BLOCK)
    return ((near, far), (far, near))


def total(part, got, mine, theirs):
    return part[mine, :].astype(f32) + got[theirs, :].astype(f32)


class Refs:
    pass


def kernel_call(kernel, name, tables, dense=(), loaded=(), buffers=(), outs=(), stored=(), packed=(), scratch=(), grant=GRANT):
    hbm = pl.BlockSpec(memory_space=pltpu.HBM)
    where = pl.BlockSpec(memory_space=pl.ANY)
    counts = [len(x) for x in (dense, loaded, buffers, outs, stored, packed, scratch, loaded, stored)]

    def run(tab, *refs):
        r = Refs()
        parts = []
        for count in counts:
            parts.append(refs[:count])
            refs = refs[count:]
        r.dense, loads, r.buffers, r.outs, saves, r.packed, r.scratch, r.loaded, r.stored = parts
        load_sems, save_sems = refs
        for n, source in enumerate(loads):
            pltpu.make_async_copy(source, r.loaded[n], load_sems.at[n]).start()

        def ready():
            for n, source in enumerate(loads):
                pltpu.make_async_copy(source, r.loaded[n], load_sems.at[n]).wait()

        def save(n):
            pltpu.make_async_copy(r.stored[n], saves[n], save_sems.at[n]).start()

        r.ready, r.save = ready, save
        kernel(tab, r)
        for n, target in enumerate(saves):
            pltpu.make_async_copy(r.stored[n], target, save_sems.at[n]).wait()

    out = pl.pallas_call(
        run,
        out_shape=(*outs, *stored, *packed),
        in_specs=[pl.BlockSpec(memory_space=pltpu.SMEM)] + whole(len(dense)) + [hbm] * len(loaded) + [where] * len(buffers),
        out_specs=(*whole(len(outs)), *[hbm] * len(stored), *[where] * len(packed)),
        scratch_shapes=[
            *scratch,
            *[pltpu.VMEM(x.shape, x.dtype) for x in loaded],
            *[pltpu.VMEM(x.shape, x.dtype) for x in stored],
            pltpu.SemaphoreType.DMA((max(len(loaded), 1),)),
            pltpu.SemaphoreType.DMA((max(len(stored), 1),)),
        ],
        compiler_params=pltpu.CompilerParams(vmem_limit_bytes=grant * 1024 * 1024),
        name=name,
    )(tables, *dense, *loaded, *buffers)
    return out


def array(shape, kind):
    return jax.ShapeDtypeStruct(shape, kind)


ROWS_F32 = array((2 * BLOCK, D), f32)
ROWS_LOW = array((2 * BLOCK, D), bf16)
ROWS_WIDE = array((2 * BLOCK, 2048), bf16)
GAIN_ROWS = array((8, D), f32)


def gain_rows_kernel(tables, buffers):
    def kernel(tab, r):
        gain, sem = r.scratch
        FIRST.move((GAIN,), tab, {GAIN: gain}, r.buffers, lambda n, b: sem, False)
        wait_all(gain, sem)
        r.outs[0][...] = jnp.transpose(gain[...].astype(f32))[:8]

    scratch = [shape_of(GAIN), pltpu.SemaphoreType.DMA]
    return kernel_call(
        kernel, "gain_rows", tables, buffers=buffers, outs=[array((8, D), f32)], scratch=scratch, grant=58
    )[0]


def att_forward(qkv, turn):
    def kernel(tab, r):
        (qkv_ref,), (att_ref,), (rot_ref, lse_ref), (att_t,) = r.dense, r.outs, r.stored, r.scratch
        cos_ref, sin_ref, start_ref = r.loaded
        q = qkv_ref[:, :, 0:128].reshape(LENGTH, 128).astype(f32)
        k = qkv_ref[:, :, 128:256].reshape(LENGTH, 128).astype(f32)
        v = qkv_ref[:, :, 256:384].reshape(LENGTH, 128)
        r.ready()
        cosine = cos_ref[...]
        sine = sin_ref[...]
        q = q * cosine + swap_halves(q) * sine
        k = k * cosine + swap_halves(k) * sine
        rot_ref[:, 0:128] = q.astype(bf16)
        rot_ref[:, 128:256] = k.astype(bf16)
        rot_ref[:, 256:384] = v
        r.save(0)
        v_t = jnp.transpose(v.astype(f32)).astype(bf16)
        for row in range(2):
            k_row = lane_mask(k, row).astype(bf16)
            for step in range(LENGTH // QB):
                first = step * QB
                keys = first + QB
                q_blk = rot_ref[first : first + QB, 0:128]
                s = mm_nt(k_row[:keys], q_blk) * score_scale
                ok = allowed_mask(start_ref[row : row + 1, first : first + QB], keys, first)
                s = jnp.where(ok, s, masked_score)
                top = jnp.max(s, axis=0, keepdims=True)
                e = jnp.exp(s - top)
                total = jnp.sum(e, axis=0, keepdims=True)
                lse_ref[row : row + 1, first : first + QB] = top + jnp.log(total)
                p = (e * (1.0 / total)).astype(bf16)
                att_t[row * 64 : row * 64 + 64, first : first + QB] = mm(v_t[row * 64 : row * 64 + 64, :keys], p)
        r.save(1)
        att_ref[...] = jnp.transpose(att_t[...]).astype(bf16).reshape(8, BLOCK, 128)

    return kernel_call(
        kernel,
        "att_forward",
        jnp.zeros((1,), jnp.int32),
        dense=(qkv,),
        loaded=turn,
        outs=[array((8, BLOCK, 128), bf16)],
        stored=[array((LENGTH, 384), bf16), array((8, LENGTH), f32)],
        scratch=[pltpu.VMEM((128, LENGTH), f32)],
    )


def att_backward(datt, rot, lse, turn):
    def kernel(tab, r):
        (datt_ref,), (out_ref,), (dk_acc, dv_acc, dq_t) = r.dense, r.outs, r.scratch
        rot_ref, lse_ref, cos_ref, sin_ref, start_ref = r.loaded
        datt = datt_ref[...].reshape(LENGTH, 128)
        dk_acc[...] = jnp.zeros_like(dk_acc)
        dv_acc[...] = jnp.zeros_like(dv_acc)
        r.ready()
        cosine = cos_ref[...]
        sine = sin_ref[...]
        q = rot_ref[:, 0:128]
        k = rot_ref[:, 128:256]
        v = rot_ref[:, 256:384]
        k_t = jnp.transpose(k.astype(f32)).astype(bf16)
        for row in range(2):
            q_row = lane_mask(q, row)
            datt_row = lane_mask(datt, row)
            for step in range(LENGTH // QB):
                first = step * QB
                keys = first + QB
                q_blk = q_row[first : first + QB]
                datt_blk = datt_row[first : first + QB]
                s = mm_nt(k[:keys], q_blk) * score_scale
                ok = allowed_mask(start_ref[row : row + 1, first : first + QB], keys, first)
                p = jnp.where(ok, jnp.exp(s - lse_ref[row : row + 1, first : first + QB]), 0.0)
                dp = mm_nt(v[:keys], datt_blk)
                delta = jnp.sum(p * dp, axis=0, keepdims=True)
                ds = (p * (dp - delta)).astype(bf16)
                dq_t[row * 64 : row * 64 + 64, first : first + QB] = mm(k_t[row * 64 : row * 64 + 64, :keys], ds)
                dk_acc[0:keys, :] += mm(ds, q_blk)
                dv_acc[0:keys, :] += mm(p.astype(bf16), datt_blk)
        dq = jnp.transpose(dq_t[...]) * score_scale
        dk = dk_acc[...] * score_scale
        out_ref[:, :, 0:128] = (dq * cosine - swap_halves(dq) * sine).astype(bf16).reshape(8, BLOCK, 128)
        out_ref[:, :, 128:256] = (dk * cosine - swap_halves(dk) * sine).astype(bf16).reshape(8, BLOCK, 128)
        out_ref[:, :, 256:384] = dv_acc[...].astype(bf16).reshape(8, BLOCK, 128)

    return kernel_call(
        kernel,
        "att_backward",
        jnp.zeros((1,), jnp.int32),
        dense=(datt,),
        loaded=(rot, lse, *turn),
        outs=[array((8, BLOCK, 384), bf16)],
        scratch=[pltpu.VMEM((LENGTH, 128), f32), pltpu.VMEM((LENGTH, 128), f32), pltpu.VMEM((128, LENGTH), f32)],
    )[0]


def qkv_forward(l, tables, gains, hidden, previous, source):
    layout, buffers = source

    def kernel(tab, r):
        gain, *below = r.dense
        rows_in, normed = r.loaded[0], r.stored[0]
        weight, sem = r.scratch
        layout.move((QKV,), tab, {QKV: weight}, r.buffers, lambda n, b: sem, False)
        r.ready()
        for mine, theirs in halves():
            rows = rows_in[mine, :]
            if below:
                down = total(*below, mine, theirs)
                r.stored[2][mine, :] = down
                rows = rows + rms_norm(down, gain[4 * l - 1 : 4 * l, :])
                r.stored[1][mine, :] = rows
            normed[mine, :] = rms_norm(rows, gain[4 * l : 4 * l + 1, :]).astype(bf16)
        for n in range(len(r.stored)):
            r.save(n)
        wait_all(weight, sem)
        for pair in range(4):
            mixed = mm(normed[...], weight[:, pair * 384 : pair * 384 + 384])
            for t in range(3):
                first, second = merge(
                    mixed[:BLOCK, t * 128 : t * 128 + 128], mixed[BLOCK:, t * 128 : t * 128 + 128]
                )
                r.outs[0][2 * pair, :, t * 128 : t * 128 + 128] = first.astype(bf16)
                r.outs[0][2 * pair + 1, :, t * 128 : t * 128 + 128] = second.astype(bf16)

    return kernel_call(
        kernel,
        "qkv_forward",
        tables,
        dense=(gains, *previous),
        loaded=(hidden,),
        buffers=buffers,
        outs=[array((8, BLOCK, 384), bf16)],
        stored=[ROWS_LOW] + ([ROWS_F32, ROWS_F32] if previous else []),
        scratch=[shape_of(QKV), pltpu.SemaphoreType.DMA],
        grant=GRANT if previous else 58,
    )


def out_forward(tables, att, source):
    layout, buffers = source

    def kernel(tab, r):
        (att_in,), (part,), (rows,), (weight, sem) = r.dense, r.outs, r.stored, r.scratch
        layout.move((OUT,), tab, {OUT: weight}, r.buffers, lambda n, b: sem, False)
        for pair in range(4):
            near, far = merge(att_in[2 * pair].astype(f32), att_in[2 * pair + 1].astype(f32))
            rows[:BLOCK, pair * 128 : pair * 128 + 128] = near.astype(bf16)
            rows[BLOCK:, pair * 128 : pair * 128 + 128] = far.astype(bf16)
        r.save(0)
        wait_all(weight, sem)
        part[...] = mm(rows[...], weight[...]).astype(bf16)

    return kernel_call(
        kernel,
        "out_forward",
        tables,
        dense=(att,),
        buffers=buffers,
        outs=[ROWS_LOW],
        stored=[array((2 * BLOCK, 512), bf16)],
        scratch=[shape_of(OUT), pltpu.SemaphoreType.DMA],
    )


def mlp_forward(l, tables, gains, branch, hidden, source):
    layout, buffers = source

    def kernel(tab, r):
        gain, part, got = r.dense
        summed, middle, normed, active, slope = r.stored
        up, down, sems = r.scratch
        targets = {UP: up, DOWN: down}
        for n, name in enumerate((UP, DOWN)):
            layout.move((name,), tab, targets, r.buffers, lambda _, b: sems.at[n], False)
        r.ready()
        for mine, theirs in halves():
            values = total(part, got, mine, theirs)
            summed[mine, :] = values
            rows = r.loaded[0][mine, :] + rms_norm(values, gain[4 * l + 1 : 4 * l + 2, :])
            middle[mine, :] = rows
            normed[mine, :] = rms_norm(rows, gain[4 * l + 2 : 4 * l + 3, :]).astype(bf16)
        for n in range(3):
            r.save(n)
        wait_all(up, sems.at[0])
        for f in range(0, 2048, 256):
            u = mm(normed[...], up[:, f : f + 256])
            phi = 0.5 * (1.0 + lax.erf(u * (0.5**0.5)))
            active[:, f : f + 256] = (u * phi).astype(bf16)
            slope[:, f : f + 256] = (phi + u * (jnp.exp(-0.5 * u * u) * 0.3989422804014327)).astype(bf16)
        for n in range(3, 5):
            r.save(n)
        wait_all(down, sems.at[1])
        for n in range(0, 1024, 256):
            r.outs[0][:, n : n + 256] = mm(active[...], down[:, n : n + 256]).astype(bf16)

    return kernel_call(
        kernel,
        "mlp_forward",
        tables,
        dense=(gains, *branch),
        loaded=(hidden,),
        buffers=buffers,
        outs=[ROWS_LOW],
        stored=[ROWS_F32, ROWS_F32, ROWS_LOW, ROWS_WIDE, ROWS_WIDE],
        scratch=[shape_of(UP), shape_of(DOWN), pltpu.SemaphoreType.DMA((2,))],
    )


def mlp_backward(l, tables, gains, grad_rows, above, down, kept, source, gain_grads):
    layout, buffers = source
    parts = len(down) == 2

    def kernel(tab, r):
        gain, gain_rows, *near = r.dense
        grad_in, active, slope, before, *rest = r.loaded
        up, down_weight, grad_up, grad_down, d_up, rows, sems = r.scratch
        (packed,) = r.packed
        weights = {UP: up, DOWN: down_weight}
        for n, name in enumerate((DOWN, UP)):
            layout.move((name,), tab, weights, r.buffers, lambda _, b: sems.at[n], False)
        wholes = {UP: grad_up, DOWN: grad_down}
        r.ready()
        r.outs[1][...] = gain_rows[...]
        for mine, theirs in halves():
            grad = grad_in[mine, :]
            if above:
                back, gain_four = rms_back(rest[0][mine, :], gain[4 * l + 4 : 4 * l + 5, :], total(*near, mine, theirs))
                grad = grad + back
                r.outs[2][mine, :] = grad
            values = total(*near, mine, theirs) if parts else rest[1][mine, :]
            back, gain_row = rms_back(values, gain[4 * l + 3 : 4 * l + 4, :], grad)
            rows[mine, :] = back.astype(bf16)
            if mine.start == 0:
                r.outs[1][4 * l + 3 : 4 * l + 4, :] = gain_row
                if above:
                    r.outs[1][4 * l + 4 : 4 * l + 5, :] = gain_four
        for f in range(0, 2048, 512):
            grad_down[f : f + 512, :] = mm_tn(active[:, f : f + 512], rows[...]).astype(bf16)
        FEED_SUM.move((DOWN,), tab, wholes, [packed], lambda _, b: sems.at[2], True)
        wait_all(down_weight, sems.at[0])
        for f in range(0, 2048, 512):
            d_active = mm_nt(rows[...], down_weight[f : f + 512, :])
            d_up[:, f : f + 512] = (d_active * slope[:, f : f + 512].astype(f32)).astype(bf16)
            grad_up[:, f : f + 512] = mm_tn(before[...], d_up[:, f : f + 512]).astype(bf16)
        FEED_SUM.move((UP,), tab, wholes, [packed], lambda _, b: sems.at[2], True)
        wait_all(up, sems.at[1])
        for n in range(0, 1024, 256):
            r.outs[0][:, n : n + 256] = mm_nt(d_up[...], up[n : n + 256, :]).astype(bf16)
        wait_all(packed, sems.at[2])

    *outs, packed = kernel_call(
        kernel,
        "mlp_backward",
        tables,
        dense=(gains, gain_grads, *(down if parts else above[:2])),
        loaded=(grad_rows, *kept, *((above[2], down[0]) if above else ())),
        buffers=buffers,
        outs=[ROWS_LOW, GAIN_ROWS] + ([ROWS_F32] if above else []),
        packed=[array(FEED_SUM.shapes[0], bf16)],
        scratch=[
            shape_of(UP),
            shape_of(DOWN),
            shape_of(UP),
            shape_of(DOWN),
            pltpu.VMEM((2 * BLOCK, 2048), bf16),
            pltpu.VMEM((2 * BLOCK, D), bf16),
            pltpu.SemaphoreType.DMA((3,)),
        ],
    )
    return packed, *outs


def out_backward(l, tables, gains, d_norm, grad_rows, kept, source, gain_grads):
    layout, buffers = source

    def kernel(tab, r):
        gain, gain_rows, d_part, d_got, *rest = r.dense
        middle, summed, att_rows, *more = r.loaded
        d_att, gain_out = r.outs
        d_middle, grad = r.stored
        weight, rows, sem = r.scratch
        grad_in = (rest + more)[0]
        layout.move((OUT,), tab, {OUT: weight}, r.buffers, lambda n, b: sem, False)
        gain_out[...] = gain_rows[...]
        r.ready()
        for mine, theirs in halves():
            back, row_two = rms_back(middle[mine, :], gain[4 * l + 2 : 4 * l + 3, :], total(d_part, d_got, mine, theirs))
            back = grad_in[mine, :] + back
            d_middle[mine, :] = back
            back, row_one = rms_back(summed[mine, :], gain[4 * l + 1 : 4 * l + 2, :], back)
            rows[mine, :] = back.astype(bf16)
            if mine.start == 0:
                gain_out[4 * l + 1 : 4 * l + 2, :] = row_one
                gain_out[4 * l + 2 : 4 * l + 3, :] = row_two
        r.save(0)
        wait_all(weight, sem)
        for pair in range(4):
            back = mm_nt(rows[...], weight[pair * 128 : pair * 128 + 128, :])
            first, second = merge(back[:BLOCK], back[BLOCK:])
            d_att[2 * pair] = first.astype(bf16)
            d_att[2 * pair + 1] = second.astype(bf16)
        grad[...] = mm_tn(att_rows[...], rows[...]).astype(bf16)
        r.save(1)

    near = l == 0
    return kernel_call(
        kernel,
        "out_backward",
        tables,
        dense=(gains, gain_grads, *d_norm) + ((grad_rows,) if near else ()),
        loaded=(*kept,) + (() if near else (grad_rows,)),
        buffers=buffers,
        outs=[array((8, BLOCK, 128), bf16), GAIN_ROWS],
        stored=[ROWS_F32, array(SHAPE[OUT], bf16)],
        scratch=[shape_of(OUT), pltpu.VMEM((2 * BLOCK, D), bf16), pltpu.SemaphoreType.DMA],
    )


def last_norm(gains, d_norm, grad_rows, hidden, gain_grads):
    def kernel(tab, r):
        gain, gain_rows, d_part, d_got = r.dense
        grad_in, entered = r.loaded
        r.ready()
        mine, theirs = halves()[0]
        back, row = rms_back(entered[mine, :], gain[0:1, :], total(d_part, d_got, mine, theirs))
        r.outs[0][...] = (grad_in[mine, :] + back).astype(bf16)
        r.outs[1][...] = gain_rows[...]
        r.outs[1][0:1, :] = row

    return kernel_call(
        kernel,
        "last_norm",
        jnp.zeros((1,), jnp.int32),
        dense=(gains, gain_grads, *d_norm),
        loaded=(grad_rows, hidden),
        outs=[array((BLOCK, D), bf16), GAIN_ROWS],
    )


def qkv_backward(l, tables, d_mixed, normed, source, held):
    layout, buffers = source
    pack = l == 0

    def kernel(tab, r):
        (d_in,), before = r.dense, r.loaded[0]
        weight, d_rows, sems, *grad = r.scratch
        grad = grad[0] if pack else r.stored[0]
        layout.move((QKV,), tab, {QKV: weight}, r.buffers, lambda n, b: sems.at[0], False)
        for pair in range(4):
            for t in range(3):
                a, b = merge(
                    d_in[2 * pair, :, t * 128 : t * 128 + 128].astype(f32),
                    d_in[2 * pair + 1, :, t * 128 : t * 128 + 128].astype(f32),
                )
                at = pair * 384 + t * 128
                d_rows[:BLOCK, at : at + 128] = a.astype(bf16)
                d_rows[BLOCK:, at : at + 128] = b.astype(bf16)
        r.ready()
        for f in range(0, 1536, 384):
            grad[:, f : f + 384] = mm_tn(before[...], d_rows[:, f : f + 384]).astype(bf16)
        if pack:
            wholes = {QKV: grad, OUT: r.loaded[1], QKV_ONE: r.loaded[2], OUT_ONE: r.loaded[3]}
            TAIL.move(TAIL.names, tab, wholes, r.packed, lambda n, b: sems.at[1 + b], True)
        else:
            r.save(0)
        wait_all(weight, sems.at[0])
        for n in range(0, 1024, 256):
            r.outs[0][:, n : n + 256] = mm_nt(d_rows[...], weight[n : n + 256, :]).astype(bf16)
        for n, target in enumerate(r.packed):
            wait_all(target, sems.at[1 + n])

    return kernel_call(
        kernel,
        "qkv_backward",
        tables,
        dense=(d_mixed,),
        loaded=(normed, *held),
        buffers=buffers,
        outs=[ROWS_LOW],
        stored=[] if pack else [array(SHAPE[QKV], bf16)],
        packed=[array(shape, bf16) for shape in TAIL.shapes] if pack else [],
        scratch=[shape_of(QKV), pltpu.VMEM((2 * BLOCK, 1536), bf16), pltpu.SemaphoreType.DMA((7,))]
        + ([shape_of(QKV)] if pack else []),
    )


def fold(cur, axis, phase):
    half = cur.shape[0] // 2
    return add_low(cur[:half], pair_swap(cur[half:], axis, phase))


CROSS = {
    flip: [
        (device_at(z, x, c, y), device_at((z // 2) * 2 + c, x, (z % 2) ^ flip, y))
        for z in range(4)
        for x in range(4)
        for c in range(2)
        for y in range(4)
    ]
    for flip in range(2)
}
CROSS_BACK = {flip: [(b, a) for a, b in CROSS[flip]] for flip in range(2)}


def rows_to_units(halves, zl, core):
    near = lax.ppermute(jnp.where(zl == 0, halves[0], halves[1]), ALL, CROSS[0])
    far = lax.ppermute(jnp.where(zl == 0, halves[1], halves[0]), ALL, CROSS[1])
    return jnp.where(core == 0, jnp.concatenate([near, far], axis=0), jnp.concatenate([far, near], axis=0))


def units_to_rows(units, zl, core):
    near = lax.ppermute(jnp.where(core == 0, units[:8], units[8:]), ALL, CROSS_BACK[0])
    far = lax.ppermute(jnp.where(core == 0, units[8:], units[:8]), ALL, CROSS_BACK[1])
    return jnp.where(zl == 0, jnp.stack([near, far]), jnp.stack([far, near]))


def zl_swap(x):
    return lax.ppermute(x, "zl", [(0, 1), (1, 0)])


def out_to_unit(out, zl):
    low, high = out[..., :512], out[..., 512:]
    kept = jnp.where(zl == 0, low, high)
    got = zl_swap(jnp.where(zl == 0, high, low))
    return jnp.where(zl == 0, jnp.concatenate([kept, got], axis=1), jnp.concatenate([got, kept], axis=1))


def out_to_rows(units, zl):
    top, bottom = units[:, :8], units[:, 8:]
    kept = jnp.where(zl == 0, top, bottom)
    got = zl_swap(jnp.where(zl == 0, bottom, top))
    return jnp.where(zl == 0, jnp.concatenate([kept, got], axis=-1), jnp.concatenate([got, kept], axis=-1))


def body(
    tokens,
    cotangent,
    lengths,
    w_qkv,
    w_out,
    w_up,
    w_down,
    gains,
    moment_qkv,
    moment_out,
    moment_up,
    moment_down,
    moment_gains,
    square_qkv,
    square_out,
    square_up,
    square_down,
    square_gains,
):
    core = lax.axis_index("c")
    zl = lax.axis_index("zl")
    my_z = lax.axis_index("zh") * 2 + zl
    tables = unit_tables((my_z, lax.axis_index("x"), core, lax.axis_index("y")))

    both = jnp.concatenate([lengths, other_core(lengths)], axis=0)
    ends = jnp.cumsum(both, axis=-1)
    starts = ends - both
    places = jnp.arange(LENGTH, dtype=jnp.int32)
    doc_ids = jnp.sum((places[None, :, None] >= ends[:, None, :]).astype(jnp.int32), axis=-1)
    picked = doc_ids[:, :, None] == jnp.arange(4, dtype=jnp.int32)[None, None, :]
    first_place = jnp.sum(jnp.where(picked, starts[:, None, :], 0), axis=-1)
    positions = (places[None, :] - first_place).astype(f32)
    inverse = 10000.0 ** (-jnp.arange(32, dtype=f32) / 32)
    angle = positions[:, :, None] * inverse
    cos_half = jnp.cos(angle)
    sin_half = jnp.sin(angle)
    cosine = jnp.concatenate([cos_half[0], cos_half[0], cos_half[1], cos_half[1]], axis=-1)
    sine = jnp.concatenate([-sin_half[0], sin_half[0], -sin_half[1], sin_half[1]], axis=-1)
    start_rows = jnp.concatenate([first_place, jnp.zeros((6, LENGTH), jnp.int32)], axis=0)

    qkv_halves = w_qkv.astype(bf16).reshape(LAYERS, 8, 3, 4, 2, 2, 64)
    qkv_halves = qkv_halves.transpose(5, 1, 0, 3, 2, 4, 6).reshape(2, 8, LAYERS * 1536)
    up_halves = w_up.astype(bf16).reshape(LAYERS, 8, 8, 2, 256).transpose(3, 1, 0, 2, 4).reshape(2, 8, LAYERS * 2048)
    gain_rows = gains.astype(bf16).reshape(8, 8).T
    gain_rows = jnp.broadcast_to(jnp.pad(gain_rows, ((0, 0), (0, 120)))[None], (2, 8, 128))
    units = rows_to_units(jnp.concatenate([qkv_halves, up_halves, gain_rows], axis=-1), zl, core)
    qkv_units, up_units, gain_unit = units[:, :3072], units[:, 3072:7168], units[:, 7168:]
    out_units = out_to_unit(w_out.astype(bf16), zl)
    down_units = w_down.astype(bf16).reshape(LAYERS, 2, 16, 1024).transpose(0, 2, 1, 3).reshape(LAYERS, 16, 2048)
    start_space = jnp.concatenate([qkv_units[:, :1536], out_units[0], gain_unit], axis=-1)
    later_space = jnp.concatenate(
        [up_units[:, :2048], down_units[0], qkv_units[:, 1536:], out_units[1]], axis=-1
    )
    start_space = jnp.concatenate(
        [
            space[:, a:b]
            for g in range(3)
            for space, layout in ((start_space, FIRST), (later_space, SECOND))
            for a, b in layout.cuts[g]
        ],
        axis=-1,
    )
    token_rows = tokens.reshape(BLOCK, D)
    hidden = jnp.concatenate([token_rows, other_core(token_rows)], axis=0).astype(f32)
    line = jnp.concatenate([up_units[:, 2048:], down_units[1]], axis=-1)[None]
    line_got = pair_swap(line, 2, 1)
    eight = cube_all_to_all(jnp.broadcast_to(start_space[None], (8,) + start_space.shape))
    line, line_got, eight = together(line, line_got, eight)
    line = jnp.concatenate([line, line_got], axis=0)
    edges = [0]
    for g in range(3):
        edges.append(edges[-1] + FIRST.width(g) + SECOND.width(g))
    cur = [eight[..., a:b] for a, b in zip(edges, edges[1:])]
    line, line_got, got, cosine, sine, start_rows, tables, hidden = together(
        line, pair_swap(line, 2, 0), cube_round(cur, 0), cosine, sine, start_rows, tables, hidden
    )
    line = jnp.concatenate([line, line_got], axis=0)
    cur = join(cur, got)
    got = cube_round(cur, 1)
    sizes = [FIRST.width(g) for g in range(3)]
    first = join([x[..., :n] for x, n in zip(cur, sizes)], [x[..., :n] for x, n in zip(got, sizes)])
    second = join([x[..., n:] for x, n in zip(cur, sizes)], [x[..., n:] for x, n in zip(got, sizes)])
    first_got = cube_round(first, 2)
    first_got, second = together(first_got, second)
    second_got = cube_round(second, 2)
    first_buffers = [buffer for pair in zip(first, first_got) for buffer in pair]
    gains_used = gain_rows_kernel(tables, first_buffers)

    mixed, normed = qkv_forward(0, tables, gains_used, hidden, (), (FIRST, first_buffers))
    mixed, line, second_got = together(seq_swap(mixed), line, second_got)
    feed_buffer = lax.all_gather(line, XY, axis=0, tiled=True)
    second_buffers = [buffer for pair in zip(second, second_got) for buffer in pair]
    attn_source = (FIRST, first_buffers), (SECOND, second_buffers)
    feed_source = (SECOND, second_buffers), (FEED, [feed_buffer])

    turn = cosine, sine, start_rows
    previous = ()
    kept = []
    for l in range(LAYERS):
        if previous:
            mixed, normed, hidden, down_sum = qkv_forward(l, tables, gains_used, hidden, previous, attn_source[l])
            mixed = seq_swap(mixed)
        att_mine, rot, lse = att_forward(mixed, turn)
        branch, att = out_forward(tables, seq_swap(att_mine), attn_source[l])
        branch = branch, other_core(branch)
        down, branch_sum, middle, normed_mlp, active, slope = mlp_forward(
            l, tables, gains_used, branch, hidden, feed_source[l]
        )
        down = down, other_core(down)
        kept.append((hidden, normed, rot, lse, (middle, branch_sum, att), (active, slope, normed_mlp)))
        previous, hidden = down, middle
    hidden = middle[:BLOCK] + rms_norm(down[0][:BLOCK].astype(f32) + down[1][BLOCK:].astype(f32), gains_used[7:8])
    output = hidden.astype(bf16)

    grad_rows = cotangent.reshape(BLOCK, D)
    grad_rows = jnp.concatenate([grad_rows, other_core(grad_rows)], axis=0).astype(f32)
    gain_grads = jnp.zeros((8, D), f32)
    held = ()
    scattered = [None] * LAYERS
    above = ()
    for l in reversed(range(LAYERS)):
        hidden, normed, rot, lse, kept_out, kept_mlp = kept[l]
        packed, d_norm, gain_grads, *rest = mlp_backward(
            l, tables, gains_used, grad_rows, above, down, kept_mlp, feed_source[l], gain_grads
        )
        if above:
            (grad_rows,) = rest
        packed, d_norm = together(packed, d_norm)
        scattered[l] = lax.psum_scatter(packed.reshape(1024, -1), "x", scatter_dimension=0, tiled=True).reshape(16, 16, -1)
        d_norm = d_norm, other_core(d_norm)
        d_att, gain_grads, d_middle, grad_wout = out_backward(
            l, tables, gains_used, d_norm, grad_rows, kept_out, attn_source[l], gain_grads
        )
        d_mixed = seq_swap(att_backward(seq_swap(d_att), rot, lse, turn))
        d_norm, *held = qkv_backward(l, tables, d_mixed, normed, attn_source[l], (grad_wout, *held) if l == 0 else ())
        d_norm = d_norm, other_core(d_norm)
        if l == 1:
            held = held[0], grad_wout
        grad_rows = d_middle
        above = (*d_norm, hidden)
        down = (down_sum,)
    input_grad, gain_grads = last_norm(gains_used, d_norm, grad_rows, hidden, gain_grads)

    tail = [held[0], held[2]], [held[1], held[3]]
    tail = scatter_round(*tail, 2)
    feed_zero, feed_one = scattered
    feed_one = fold(feed_one, 1, 0)

    gain_sum = gain_grads.reshape(8, 128, 8).transpose(1, 0, 2).reshape(128, 1, 64)
    gain_sum = lax.all_to_all(gain_sum, ALL, 0, 0, tiled=True)
    tail, feed_one, gain_sum = together(tail, feed_one, gain_sum)
    g_gain = jnp.sum(gain_sum, axis=0).reshape(LAYERS, 4, 8)

    tail = scatter_round(*tail, 1)
    feed_one = fold(feed_one, 1, 1)
    feed_zero = fold(feed_zero, 1, 0)
    tail, feed_zero, feed_one = together(tail, feed_zero, feed_one)
    tail = scatter_round(*tail, 0)
    feed_one = fold(feed_one, 2, 0)
    feed_zero = fold(feed_zero, 1, 1)
    tail, feed_zero, feed_one = together(tail, feed_zero, feed_one)
    feed_one = fold(feed_one, 2, 1)[0]
    feed_zero = fold(fold(feed_zero, 2, 0), 2, 1)[0]
    tail_own = jnp.concatenate([jnp.concatenate(x, axis=-1) for x in tail], axis=0)
    tail_own, feed_zero, feed_one = together(cube_all_to_all(tail_own), feed_zero, feed_one)
    tail_own = jnp.sum(tail_own.astype(f32), axis=0).astype(bf16)

    g_out_units = jnp.stack([tail_own[:, 1536:2048], tail_own[:, 3584:]])
    g_down = jnp.stack([feed_zero[:, 2048:], feed_one[:, 2048:]])
    g_down = g_down.reshape(LAYERS, 16, 2, 1024).transpose(0, 2, 1, 3).reshape(LAYERS, 32, 1024).astype(f32)
    both = jnp.concatenate(
        [tail_own[:, :1536], tail_own[:, 2048:3584], feed_zero[:, :2048], feed_one[:, :2048]], axis=-1
    )
    both, g_out_units = together(both, g_out_units)
    g_out = out_to_rows(g_out_units, zl).astype(f32)
    both = units_to_rows(both, zl, core).astype(f32)
    g_qkv = both[..., :3072].reshape(2, 8, LAYERS, 4, 3, 2, 64).transpose(2, 1, 4, 3, 5, 0, 6).reshape(LAYERS, 8, 3 * D)
    g_up = both[..., 3072:].reshape(2, 8, LAYERS, 8, 256).transpose(2, 1, 3, 0, 4).reshape(LAYERS, 8, FF)

    upd_qkv = adam_update(w_qkv, moment_qkv, square_qkv, g_qkv, rate_matrix, weight_decay)
    upd_out = adam_update(w_out, moment_out, square_out, g_out, rate_matrix, weight_decay)
    upd_up = adam_update(w_up, moment_up, square_up, g_up, rate_matrix, weight_decay)
    upd_down = adam_update(w_down, moment_down, square_down, g_down, rate_matrix, weight_decay)
    upd_gains = adam_update(gains, moment_gains, square_gains, g_gain, rate_gain, 0.0)
    updates = (upd_qkv, upd_out, upd_up, upd_down, upd_gains)
    return (
        output.reshape(BLOCK, 1, D),
        input_grad.reshape(BLOCK, 1, D),
        *(u[0] for u in updates),
        *(u[1] for u in updates),
        *(u[2] for u in updates),
        *(u[0].astype(bf16) for u in updates),
    )


def solution(mesh):
    fine = Mesh(mesh.devices.reshape(2, 4, 2, 4, 2), ("zh", "x", "c", "y", "zl"))
    tokens_spec = P(SEQ, DP, None)
    rows_spec = P(None, DP + SEQ, None)
    gains_spec = P(None, None, DP + SEQ)
    masters = (rows_spec,) * 4 + (gains_spec,)
    return jax.shard_map(
        body,
        mesh=fine,
        in_specs=(tokens_spec, tokens_spec, P(DP, None)) + masters * 3,
        out_specs=(tokens_spec, tokens_spec) + masters * 4,
        check_vma=False,
    )
```

```python
import jax
import jax.numpy as jnp
from jax import lax
from jax.experimental import pallas as pl
from jax.experimental.pallas import tpu as pltpu
from jax.sharding import Mesh
from jax.sharding import PartitionSpec as P

D = 1024
HEADS = 16
HEAD_DIM = 64
FF = 4096
LAYERS = 2
STEP = 5
LENGTH = 1024
BLOCK = 128
QB = 256
GRANT = 48

norm_eps = 1e-05
beta_first = 0.9
beta_second = 0.95
adam_eps = 1e-08
weight_decay = 0.1
rate_matrix = 0.04
rate_gain = 0.4
masked_score = -1e30
score_scale = HEAD_DIM ** (-0.5)

bf16 = jnp.bfloat16
f32 = jnp.float32
SEQ = ("y", "zl")
DP = ("zh", "x", "c")
ZAX = ("zh", "zl")
XY = ("x", "y")
ALL = ("zh", "x", "c", "y", "zl")


def dot(a, b, dims):
    return lax.dot_general(a, b, (dims, ((), ())), preferred_element_type=f32)


def mm(a, b):
    return dot(a, b, ((1,), (0,)))


def mm_nt(a, b):
    return dot(a, b, ((1,), (1,)))


def mm_tn(a, b):
    return dot(a, b, ((0,), (0,)))


def swap_halves(x):
    lane = lax.broadcasted_iota(jnp.int32, x.shape, 1)
    return jnp.where((lane % 64) < 32, pltpu.roll(x, 96, 1), pltpu.roll(x, 32, 1))


def lane_mask(x, row):
    lane = lax.broadcasted_iota(jnp.int32, x.shape, 1)
    return jnp.where((lane // 64) == row, x, jnp.zeros_like(x))


def allowed_mask(start_row, keys, first_query):
    key = lax.broadcasted_iota(jnp.int32, (keys, QB), 0)
    query = lax.broadcasted_iota(jnp.int32, (keys, QB), 1) + first_query
    return (key >= start_row) & (key <= query)


def whole(count):
    return [pl.BlockSpec(memory_space=pltpu.VMEM)] * count


def rms_scale(values):
    return lax.rsqrt(jnp.mean(values * values, axis=-1, keepdims=True) + norm_eps)


def rms_norm(values, gain_row):
    return values * rms_scale(values) * gain_row


def rms_back(values, gain_row, grad):
    scale = rms_scale(values)
    unit = values * scale
    scaled = grad * gain_row
    inner = jnp.mean(scaled * unit, axis=-1, keepdims=True)
    return scale * (scaled - unit * inner), jnp.sum(grad * unit, axis=0, keepdims=True)


def adam_update(master, moment_one, moment_two, gradient, rate, decay):
    moment_new = beta_first * moment_one + (1.0 - beta_first) * gradient
    square_new = beta_second * moment_two + (1.0 - beta_second) * gradient * gradient
    moment_hat = moment_new / (1.0 - beta_first**STEP)
    square_hat = square_new / (1.0 - beta_second**STEP)
    updated = master - rate * (moment_hat / (jnp.sqrt(square_hat) + adam_eps) + decay * master)
    return (updated, moment_new, square_new)


def other_core(x):
    return lax.ppermute(x, "c", [(0, 1), (1, 0)])


def seq_swap(x):
    return lax.all_to_all(x, SEQ, 0, 0, tiled=True)


CUBE, PLANE, AXIS = (0, 1, 2), (3,), (4,)
QKV, OUT, UP, DOWN, GAIN, QKV_ONE, OUT_ONE = "qkv", "out", "up", "down", "gain", "qkv1", "out1"
WIDTH = {QKV: 1536, OUT: 512, UP: 2048, DOWN: 2048, GAIN: 128, QKV_ONE: 1536, OUT_ONE: 512}
SHAPE = {QKV: (1024, 1536), OUT: (512, 1024), UP: (1024, 2048), DOWN: (2048, 1024), GAIN: (1024, 128)}


def place(i):
    return (i // 64) * 2 + i % 2, (i // 16) % 4, (i // 8) % 2, (i // 2) % 4


def device_at(z, x, c, y):
    return (((z // 2) * 4 + x) * 2 + c) * 8 + y * 2 + z % 2


def pairs(axis, phase):
    found = []
    for i in range(128):
        z, x, c, y = place(i)
        mask = 3 if (c if phase else 1 - c) else 1
        x, y, z = (x ^ mask, y, z) if axis == 0 else (x, y ^ mask, z) if axis == 1 else (x, y, z ^ mask)
        found.append((i, device_at(z, x, c, y)))
    return found


PAIRS = {(axis, phase): pairs(axis, phase) for axis in range(3) for phase in range(2)}


def pair_swap(x, axis, phase):
    return lax.ppermute(x, ALL, PAIRS[axis, phase])


def add_low(a, b):
    return (a.astype(f32) + b.astype(f32)).astype(bf16)


def cube_groups():
    found = {}
    for i in range(128):
        z, x, c, y = place(i)
        shift, mask = (0, 1) if c else (1, 3)
        rank = ((x >> shift) & 1) * 4 + ((y >> shift) & 1) * 2 + ((z >> shift) & 1)
        key = (c,) + tuple(min(v, v ^ mask) for v in (x, y, z))
        found.setdefault(key, [0] * 8)[rank] = i
    return list(found.values())


CUBES = cube_groups()


def cube_all_to_all(x):
    return lax.all_to_all(x, ALL, 0, 0, axis_index_groups=CUBES, tiled=True)


AXES = {0: (0, 1, 2), 1: (1, 2, 0), 2: (2, 0, 1), 5: (0, 2, 1)}


def cube_round(cur, k, orders=(0, 1, 2)):
    return [pair_swap(x, AXES[g][k], 1) for x, g in zip(cur, orders)]


def join(cur, got):
    return [jnp.concatenate([x, y], axis=0) for x, y in zip(cur, got)]


def scatter_round(keep, send, k):
    got = cube_round(send, k, (0, 5))
    half = keep[0].shape[0] // 2
    send = [add_low(x[half:], y[half:]) for x, y in zip(keep, got)]
    return [add_low(x[:half], y[:half]) for x, y in zip(keep, got)], send


def together(*values):
    return lax.optimization_barrier(values)


def unit_tables(mine):
    my_z, my_x, core, my_y = mine
    first = jnp.where(core == 0, 3, 1)
    last = jnp.where(core == 0, 1, 3)
    shift = jnp.where(core == 0, 1, 0)
    p = jnp.arange(64, dtype=jnp.int32)
    rows = []
    for g in range(7):
        if g in AXES:
            at = [my_x, my_y, my_z]
            for k, axis in enumerate(AXES[g]):
                at[axis] = at[axis] ^ (((p >> (3 + k)) & 1) * last)
            for axis in range(3):
                differs = ((at[axis] >> shift) & 1) ^ ((p >> (2 - axis)) & 1)
                at[axis] = at[axis] ^ (differs * first)
            x, y, z = at
        elif g == 6:
            x, y = p >> 4, my_y ^ ((p & 1) * last) ^ (((p >> 1) & 1) * first)
            z = my_z ^ (((p >> 2) & 1) * last) ^ (((p >> 3) & 1) * first)
        else:
            x, y = (p >> 4, (p >> 2) & 3) if g == 3 else (p >> 4, my_y ^ (((p >> 2) & 1) * last) ^ (((p >> 3) & 1) * first))
            z = my_z ^ ((p & 1) * last) ^ (((p >> 1) & 1) * first)
        zh, zl = z >> 1, z & 1
        rows += [
            (((zh * 4 + x) * 2 + zl) * 4 + y) * 16,
            ((zh * 4 + x) * 4 + y) * 16,
            zl * 512,
            (((zh * 4 + x) * 4 + y) * 2 + zl) * 32,
        ]
    return jnp.stack(rows).astype(jnp.int32)


def segments(names, bounds):
    pieces = []
    start = 0
    for name in names:
        for part in range(2 if name == DOWN else 1):
            width = 1024 if name == DOWN else WIDTH[name]
            pieces.append((name, start, width, 16 * part))
            start += width
    found = []
    for ranges in bounds:
        group = []
        at = 0
        for a, b in ranges:
            for name, first, width, extra in pieces:
                lo, hi = max(a, first), min(b, first + width)
                if lo < hi:
                    group.append((name, at + lo - a, lo - first, hi - lo, extra))
            at += b - a
        found.append(group)
    return found


def whole_slice(tab, ref, name, group, p, column, count, extra):
    if name in (OUT, OUT_ONE):
        row = pl.multiple_of(tab[4 * group + 1, p], 16)
        col = pl.multiple_of(tab[4 * group + 2, p] + column, 128)
        return ref.at[pl.ds(row, 16), pl.ds(col, count)]
    if name == DOWN:
        row = pl.multiple_of(tab[4 * group + 3, p] + extra, 16)
    else:
        row = pl.multiple_of(tab[4 * group, p], 16)
    return ref.at[pl.ds(row, 16), pl.ds(column, count)]


class Layout:
    def __init__(self, names, cuts, order, per):
        self.names, self.cuts, self.order, self.per = names, cuts, order, per
        self.plan = segments(names, cuts)
        self.shapes = [(64 // per, 16, self.width(g)) for g in range(len(cuts)) for _ in range(per)]

    def width(self, g):
        return sum(b - a for a, b in self.cuts[g])

    def move(self, names, tab, wholes, buffers, sem_of, store):
        def step(i, carry):
            for g, group in enumerate(self.plan):
                for part in range(self.per):
                    at_buffer = g * self.per + part
                    for name, at, column, count, extra in group:
                        if name not in names:
                            continue
                        piece = buffers[at_buffer].at[i, :, pl.ds(at, count)]
                        place_in = i + part * (64 // self.per)
                        own = whole_slice(tab, wholes[name], name, self.order[g], place_in, column, count, extra)
                        ends = (own, piece) if store else (piece, own)
                        pltpu.make_async_copy(*ends, sem_of(name, at_buffer)).start()
            return carry

        lax.fori_loop(0, 64 // self.per, step, 0)


FIRST = Layout((QKV, OUT, GAIN), (((0, 768),), ((768, 1536),), ((1536, 2176),)), CUBE, 2)
SECOND = Layout(
    (UP, DOWN, QKV, OUT),
    (((0, 1408), (4096, 4736)), ((1408, 2816), (4736, 5376)), ((2816, 4096), (5376, 6144))),
    CUBE,
    2,
)
FEED = Layout((UP, DOWN), (((0, 4096),),), PLANE, 1)
FEED_SUMS = tuple(Layout((UP, DOWN), (((0, 4096),),), order, 1) for order in ((6,), AXIS))
TAIL = Layout((QKV, OUT, QKV_ONE, OUT_ONE), (((0, 2048),), ((2048, 4096),)), (0, 5), 2)


def wait_all(ref, sem):
    pltpu.make_async_copy(ref, ref, sem).wait()


def shape_of(name):
    return pltpu.VMEM(SHAPE[name], bf16)


def merge(a, b):
    low = lax.broadcasted_iota(jnp.int32, a.shape, 1) < 64
    return jnp.where(low, a, pltpu.roll(b, 64, 1)), jnp.where(low, pltpu.roll(a, 64, 1), b)


def halves():
    near, far = slice(0, BLOCK), slice(BLOCK, 2 * BLOCK)
    return ((near, far), (far, near))


def total(part, got, mine, theirs):
    return part[mine, :].astype(f32) + got[theirs, :].astype(f32)


class Refs:
    pass


def kernel_call(kernel, name, tables, dense=(), loaded=(), buffers=(), outs=(), stored=(), packed=(), scratch=(), grant=GRANT):
    hbm = pl.BlockSpec(memory_space=pltpu.HBM)
    where = pl.BlockSpec(memory_space=pl.ANY)
    counts = [len(x) for x in (dense, loaded, buffers, outs, stored, packed, scratch, loaded, stored)]

    def run(tab, *refs):
        r = Refs()
        parts = []
        for count in counts:
            parts.append(refs[:count])
            refs = refs[count:]
        r.dense, loads, r.buffers, r.outs, saves, r.packed, r.scratch, r.loaded, r.stored = parts
        load_sems, save_sems = refs
        for n, source in enumerate(loads):
            pltpu.make_async_copy(source, r.loaded[n], load_sems.at[n]).start()

        def ready():
            for n, source in enumerate(loads):
                pltpu.make_async_copy(source, r.loaded[n], load_sems.at[n]).wait()

        def save(n):
            pltpu.make_async_copy(r.stored[n], saves[n], save_sems.at[n]).start()

        r.ready, r.save = ready, save
        kernel(tab, r)
        for n, target in enumerate(saves):
            pltpu.make_async_copy(r.stored[n], target, save_sems.at[n]).wait()

    out = pl.pallas_call(
        run,
        out_shape=(*outs, *stored, *packed),
        in_specs=[pl.BlockSpec(memory_space=pltpu.SMEM)] + whole(len(dense)) + [hbm] * len(loaded) + [where] * len(buffers),
        out_specs=(*whole(len(outs)), *[hbm] * len(stored), *[where] * len(packed)),
        scratch_shapes=[
            *scratch,
            *[pltpu.VMEM(x.shape, x.dtype) for x in loaded],
            *[pltpu.VMEM(x.shape, x.dtype) for x in stored],
            pltpu.SemaphoreType.DMA((max(len(loaded), 1),)),
            pltpu.SemaphoreType.DMA((max(len(stored), 1),)),
        ],
        compiler_params=pltpu.CompilerParams(vmem_limit_bytes=grant * 1024 * 1024),
        name=name,
    )(tables, *dense, *loaded, *buffers)
    return out


def array(shape, kind):
    return jax.ShapeDtypeStruct(shape, kind)


ROWS_F32 = array((2 * BLOCK, D), f32)
ROWS_LOW = array((2 * BLOCK, D), bf16)
ROWS_WIDE = array((2 * BLOCK, 2048), bf16)
GAIN_ROWS = array((8, D), f32)


def gain_rows_kernel(tables, buffers):
    def kernel(tab, r):
        gain, sem = r.scratch
        FIRST.move((GAIN,), tab, {GAIN: gain}, r.buffers, lambda n, b: sem, False)
        wait_all(gain, sem)
        r.outs[0][...] = jnp.transpose(gain[...].astype(f32))[:8]

    scratch = [shape_of(GAIN), pltpu.SemaphoreType.DMA]
    return kernel_call(
        kernel, "gain_rows", tables, buffers=buffers, outs=[array((8, D), f32)], scratch=scratch, grant=58
    )[0]


def att_forward(qkv, turn):
    def kernel(tab, r):
        (qkv_ref,), (att_ref,), (rot_ref, lse_ref), (att_t,) = r.dense, r.outs, r.stored, r.scratch
        cos_ref, sin_ref, start_ref = r.loaded
        q = qkv_ref[:, :, 0:128].reshape(LENGTH, 128).astype(f32)
        k = qkv_ref[:, :, 128:256].reshape(LENGTH, 128).astype(f32)
        v = qkv_ref[:, :, 256:384].reshape(LENGTH, 128)
        r.ready()
        cosine = cos_ref[...]
        sine = sin_ref[...]
        q = q * cosine + swap_halves(q) * sine
        k = k * cosine + swap_halves(k) * sine
        rot_ref[:, 0:128] = q.astype(bf16)
        rot_ref[:, 128:256] = k.astype(bf16)
        rot_ref[:, 256:384] = v
        r.save(0)
        v_t = jnp.transpose(v.astype(f32)).astype(bf16)
        for row in range(2):
            k_row = lane_mask(k, row).astype(bf16)
            for step in range(LENGTH // QB):
                first = step * QB
                keys = first + QB
                q_blk = rot_ref[first : first + QB, 0:128]
                s = mm_nt(k_row[:keys], q_blk) * score_scale
                ok = allowed_mask(start_ref[row : row + 1, first : first + QB], keys, first)
                s = jnp.where(ok, s, masked_score)
                top = jnp.max(s, axis=0, keepdims=True)
                e = jnp.exp(s - top)
                total = jnp.sum(e, axis=0, keepdims=True)
                lse_ref[row : row + 1, first : first + QB] = top + jnp.log(total)
                p = (e * (1.0 / total)).astype(bf16)
                att_t[row * 64 : row * 64 + 64, first : first + QB] = mm(v_t[row * 64 : row * 64 + 64, :keys], p)
        r.save(1)
        att_ref[...] = jnp.transpose(att_t[...]).astype(bf16).reshape(8, BLOCK, 128)

    return kernel_call(
        kernel,
        "att_forward",
        jnp.zeros((1,), jnp.int32),
        dense=(qkv,),
        loaded=turn,
        outs=[array((8, BLOCK, 128), bf16)],
        stored=[array((LENGTH, 384), bf16), array((8, LENGTH), f32)],
        scratch=[pltpu.VMEM((128, LENGTH), f32)],
    )


def att_backward(datt, rot, lse, turn):
    def kernel(tab, r):
        (datt_ref,), (out_ref,), (dk_acc, dv_acc, dq_t) = r.dense, r.outs, r.scratch
        rot_ref, lse_ref, cos_ref, sin_ref, start_ref = r.loaded
        datt = datt_ref[...].reshape(LENGTH, 128)
        dk_acc[...] = jnp.zeros_like(dk_acc)
        dv_acc[...] = jnp.zeros_like(dv_acc)
        r.ready()
        cosine = cos_ref[...]
        sine = sin_ref[...]
        q = rot_ref[:, 0:128]
        k = rot_ref[:, 128:256]
        v = rot_ref[:, 256:384]
        k_t = jnp.transpose(k.astype(f32)).astype(bf16)
        for row in range(2):
            q_row = lane_mask(q, row)
            datt_row = lane_mask(datt, row)
            for step in range(LENGTH // QB):
                first = step * QB
                keys = first + QB
                q_blk = q_row[first : first + QB]
                datt_blk = datt_row[first : first + QB]
                s = mm_nt(k[:keys], q_blk) * score_scale
                ok = allowed_mask(start_ref[row : row + 1, first : first + QB], keys, first)
                p = jnp.where(ok, jnp.exp(s - lse_ref[row : row + 1, first : first + QB]), 0.0)
                dp = mm_nt(v[:keys], datt_blk)
                delta = jnp.sum(p * dp, axis=0, keepdims=True)
                ds = (p * (dp - delta)).astype(bf16)
                dq_t[row * 64 : row * 64 + 64, first : first + QB] = mm(k_t[row * 64 : row * 64 + 64, :keys], ds)
                dk_acc[0:keys, :] += mm(ds, q_blk)
                dv_acc[0:keys, :] += mm(p.astype(bf16), datt_blk)
        dq = jnp.transpose(dq_t[...]) * score_scale
        dk = dk_acc[...] * score_scale
        out_ref[:, :, 0:128] = (dq * cosine - swap_halves(dq) * sine).astype(bf16).reshape(8, BLOCK, 128)
        out_ref[:, :, 128:256] = (dk * cosine - swap_halves(dk) * sine).astype(bf16).reshape(8, BLOCK, 128)
        out_ref[:, :, 256:384] = dv_acc[...].astype(bf16).reshape(8, BLOCK, 128)

    return kernel_call(
        kernel,
        "att_backward",
        jnp.zeros((1,), jnp.int32),
        dense=(datt,),
        loaded=(rot, lse, *turn),
        outs=[array((8, BLOCK, 384), bf16)],
        scratch=[pltpu.VMEM((LENGTH, 128), f32), pltpu.VMEM((LENGTH, 128), f32), pltpu.VMEM((128, LENGTH), f32)],
    )[0]


def qkv_forward(l, tables, gains, hidden, previous, source):
    layout, buffers = source

    def kernel(tab, r):
        gain, *below = r.dense
        rows_in, normed = r.loaded[0], r.stored[0]
        weight, sem = r.scratch
        layout.move((QKV,), tab, {QKV: weight}, r.buffers, lambda n, b: sem, False)
        r.ready()
        for mine, theirs in halves():
            rows = rows_in[mine, :]
            if below:
                down = total(*below, mine, theirs)
                r.stored[2][mine, :] = down
                rows = rows + rms_norm(down, gain[4 * l - 1 : 4 * l, :])
                r.stored[1][mine, :] = rows
            normed[mine, :] = rms_norm(rows, gain[4 * l : 4 * l + 1, :]).astype(bf16)
        for n in range(len(r.stored)):
            r.save(n)
        wait_all(weight, sem)
        for pair in range(4):
            mixed = mm(normed[...], weight[:, pair * 384 : pair * 384 + 384])
            for t in range(3):
                first, second = merge(
                    mixed[:BLOCK, t * 128 : t * 128 + 128], mixed[BLOCK:, t * 128 : t * 128 + 128]
                )
                r.outs[0][2 * pair, :, t * 128 : t * 128 + 128] = first.astype(bf16)
                r.outs[0][2 * pair + 1, :, t * 128 : t * 128 + 128] = second.astype(bf16)

    return kernel_call(
        kernel,
        "qkv_forward",
        tables,
        dense=(gains, *previous),
        loaded=(hidden,),
        buffers=buffers,
        outs=[array((8, BLOCK, 384), bf16)],
        stored=[ROWS_LOW] + ([ROWS_F32, ROWS_F32] if previous else []),
        scratch=[shape_of(QKV), pltpu.SemaphoreType.DMA],
        grant=GRANT if previous else 58,
    )


def out_forward(tables, att, source):
    layout, buffers = source

    def kernel(tab, r):
        (att_in,), (part,), (rows,), (weight, sem) = r.dense, r.outs, r.stored, r.scratch
        layout.move((OUT,), tab, {OUT: weight}, r.buffers, lambda n, b: sem, False)
        for pair in range(4):
            near, far = merge(att_in[2 * pair].astype(f32), att_in[2 * pair + 1].astype(f32))
            rows[:BLOCK, pair * 128 : pair * 128 + 128] = near.astype(bf16)
            rows[BLOCK:, pair * 128 : pair * 128 + 128] = far.astype(bf16)
        r.save(0)
        wait_all(weight, sem)
        part[...] = mm(rows[...], weight[...]).astype(bf16)

    return kernel_call(
        kernel,
        "out_forward",
        tables,
        dense=(att,),
        buffers=buffers,
        outs=[ROWS_LOW],
        stored=[array((2 * BLOCK, 512), bf16)],
        scratch=[shape_of(OUT), pltpu.SemaphoreType.DMA],
    )


def mlp_forward(l, tables, gains, branch, hidden, source):
    layout, buffers = source

    def kernel(tab, r):
        gain, part, got = r.dense
        summed, middle, normed, active, slope = r.stored
        up, down, sems = r.scratch
        targets = {UP: up, DOWN: down}
        for n, name in enumerate((UP, DOWN)):
            layout.move((name,), tab, targets, r.buffers, lambda _, b: sems.at[n], False)
        r.ready()
        for mine, theirs in halves():
            values = total(part, got, mine, theirs)
            summed[mine, :] = values
            rows = r.loaded[0][mine, :] + rms_norm(values, gain[4 * l + 1 : 4 * l + 2, :])
            middle[mine, :] = rows
            normed[mine, :] = rms_norm(rows, gain[4 * l + 2 : 4 * l + 3, :]).astype(bf16)
        for n in range(3):
            r.save(n)
        wait_all(up, sems.at[0])
        for f in range(0, 2048, 256):
            u = mm(normed[...], up[:, f : f + 256])
            phi = 0.5 * (1.0 + lax.erf(u * (0.5**0.5)))
            active[:, f : f + 256] = (u * phi).astype(bf16)
            slope[:, f : f + 256] = (phi + u * (jnp.exp(-0.5 * u * u) * 0.3989422804014327)).astype(bf16)
        for n in range(3, 5):
            r.save(n)
        wait_all(down, sems.at[1])
        for n in range(0, 1024, 256):
            r.outs[0][:, n : n + 256] = mm(active[...], down[:, n : n + 256]).astype(bf16)

    return kernel_call(
        kernel,
        "mlp_forward",
        tables,
        dense=(gains, *branch),
        loaded=(hidden,),
        buffers=buffers,
        outs=[ROWS_LOW],
        stored=[ROWS_F32, ROWS_F32, ROWS_LOW, ROWS_WIDE, ROWS_WIDE],
        scratch=[shape_of(UP), shape_of(DOWN), pltpu.SemaphoreType.DMA((2,))],
    )


def mlp_backward(l, tables, gains, grad_rows, above, down, kept, source, gain_grads):
    layout, buffers = source
    parts = len(down) == 2

    def kernel(tab, r):
        gain, gain_rows, *near = r.dense
        grad_in, active, slope, before, *rest = r.loaded
        up, down_weight, grad_up, grad_down, d_up, rows, sems = r.scratch
        (packed,) = r.packed
        weights = {UP: up, DOWN: down_weight}
        for n, name in enumerate((DOWN, UP)):
            layout.move((name,), tab, weights, r.buffers, lambda _, b: sems.at[n], False)
        wholes = {UP: grad_up, DOWN: grad_down}
        r.ready()
        r.outs[1][...] = gain_rows[...]
        for mine, theirs in halves():
            grad = grad_in[mine, :]
            if above:
                back, gain_four = rms_back(rest[0][mine, :], gain[4 * l + 4 : 4 * l + 5, :], total(*near, mine, theirs))
                grad = grad + back
                r.outs[2][mine, :] = grad
            values = total(*near, mine, theirs) if parts else rest[1][mine, :]
            back, gain_row = rms_back(values, gain[4 * l + 3 : 4 * l + 4, :], grad)
            rows[mine, :] = back.astype(bf16)
            if mine.start == 0:
                r.outs[1][4 * l + 3 : 4 * l + 4, :] = gain_row
                if above:
                    r.outs[1][4 * l + 4 : 4 * l + 5, :] = gain_four
        for f in range(0, 2048, 512):
            grad_down[f : f + 512, :] = mm_tn(active[:, f : f + 512], rows[...]).astype(bf16)
        FEED_SUMS[l].move((DOWN,), tab, wholes, [packed], lambda _, b: sems.at[2], True)
        wait_all(down_weight, sems.at[0])
        for f in range(0, 2048, 512):
            d_active = mm_nt(rows[...], down_weight[f : f + 512, :])
            d_up[:, f : f + 512] = (d_active * slope[:, f : f + 512].astype(f32)).astype(bf16)
            grad_up[:, f : f + 512] = mm_tn(before[...], d_up[:, f : f + 512]).astype(bf16)
        FEED_SUMS[l].move((UP,), tab, wholes, [packed], lambda _, b: sems.at[2], True)
        wait_all(up, sems.at[1])
        for n in range(0, 1024, 256):
            r.outs[0][:, n : n + 256] = mm_nt(d_up[...], up[n : n + 256, :]).astype(bf16)
        wait_all(packed, sems.at[2])

    *outs, packed = kernel_call(
        kernel,
        "mlp_backward",
        tables,
        dense=(gains, gain_grads, *(down if parts else above[:2])),
        loaded=(grad_rows, *kept, *((above[2], down[0]) if above else ())),
        buffers=buffers,
        outs=[ROWS_LOW, GAIN_ROWS] + ([ROWS_F32] if above else []),
        packed=[array(FEED_SUMS[l].shapes[0], bf16)],
        scratch=[
            shape_of(UP),
            shape_of(DOWN),
            shape_of(UP),
            shape_of(DOWN),
            pltpu.VMEM((2 * BLOCK, 2048), bf16),
            pltpu.VMEM((2 * BLOCK, D), bf16),
            pltpu.SemaphoreType.DMA((3,)),
        ],
    )
    return packed, *outs


def out_backward(l, tables, gains, d_norm, grad_rows, kept, source, gain_grads):
    layout, buffers = source

    def kernel(tab, r):
        gain, gain_rows, d_part, d_got, *rest = r.dense
        middle, summed, att_rows, *more = r.loaded
        d_att, gain_out = r.outs
        d_middle, grad = r.stored
        weight, rows, sem = r.scratch
        grad_in = (rest + more)[0]
        layout.move((OUT,), tab, {OUT: weight}, r.buffers, lambda n, b: sem, False)
        gain_out[...] = gain_rows[...]
        r.ready()
        for mine, theirs in halves():
            back, row_two = rms_back(middle[mine, :], gain[4 * l + 2 : 4 * l + 3, :], total(d_part, d_got, mine, theirs))
            back = grad_in[mine, :] + back
            d_middle[mine, :] = back
            back, row_one = rms_back(summed[mine, :], gain[4 * l + 1 : 4 * l + 2, :], back)
            rows[mine, :] = back.astype(bf16)
            if mine.start == 0:
                gain_out[4 * l + 1 : 4 * l + 2, :] = row_one
                gain_out[4 * l + 2 : 4 * l + 3, :] = row_two
        r.save(0)
        wait_all(weight, sem)
        for pair in range(4):
            back = mm_nt(rows[...], weight[pair * 128 : pair * 128 + 128, :])
            first, second = merge(back[:BLOCK], back[BLOCK:])
            d_att[2 * pair] = first.astype(bf16)
            d_att[2 * pair + 1] = second.astype(bf16)
        grad[...] = mm_tn(att_rows[...], rows[...]).astype(bf16)
        r.save(1)

    near = l == 0
    return kernel_call(
        kernel,
        "out_backward",
        tables,
        dense=(gains, gain_grads, *d_norm) + ((grad_rows,) if near else ()),
        loaded=(*kept,) + (() if near else (grad_rows,)),
        buffers=buffers,
        outs=[array((8, BLOCK, 128), bf16), GAIN_ROWS],
        stored=[ROWS_F32, array(SHAPE[OUT], bf16)],
        scratch=[shape_of(OUT), pltpu.VMEM((2 * BLOCK, D), bf16), pltpu.SemaphoreType.DMA],
    )


def last_norm(gains, d_norm, grad_rows, hidden, gain_grads):
    def kernel(tab, r):
        gain, gain_rows, d_part, d_got = r.dense
        grad_in, entered = r.loaded
        r.ready()
        mine, theirs = halves()[0]
        back, row = rms_back(entered[mine, :], gain[0:1, :], total(d_part, d_got, mine, theirs))
        r.outs[0][...] = (grad_in[mine, :] + back).astype(bf16)
        r.outs[1][...] = gain_rows[...]
        r.outs[1][0:1, :] = row

    return kernel_call(
        kernel,
        "last_norm",
        jnp.zeros((1,), jnp.int32),
        dense=(gains, gain_grads, *d_norm),
        loaded=(grad_rows, hidden),
        outs=[array((BLOCK, D), bf16), GAIN_ROWS],
    )


def qkv_backward(l, tables, d_mixed, normed, source, held):
    layout, buffers = source
    pack = l == 0

    def kernel(tab, r):
        (d_in,), before = r.dense, r.loaded[0]
        weight, d_rows, sems, *grad = r.scratch
        grad = grad[0] if pack else r.stored[0]
        layout.move((QKV,), tab, {QKV: weight}, r.buffers, lambda n, b: sems.at[0], False)
        for pair in range(4):
            for t in range(3):
                a, b = merge(
                    d_in[2 * pair, :, t * 128 : t * 128 + 128].astype(f32),
                    d_in[2 * pair + 1, :, t * 128 : t * 128 + 128].astype(f32),
                )
                at = pair * 384 + t * 128
                d_rows[:BLOCK, at : at + 128] = a.astype(bf16)
                d_rows[BLOCK:, at : at + 128] = b.astype(bf16)
        r.ready()
        for f in range(0, 1536, 384):
            grad[:, f : f + 384] = mm_tn(before[...], d_rows[:, f : f + 384]).astype(bf16)
        if pack:
            wholes = {QKV: grad, OUT: r.loaded[1], QKV_ONE: r.loaded[2], OUT_ONE: r.loaded[3]}
            TAIL.move(TAIL.names, tab, wholes, r.packed, lambda n, b: sems.at[1 + b], True)
        else:
            r.save(0)
        wait_all(weight, sems.at[0])
        for n in range(0, 1024, 256):
            r.outs[0][:, n : n + 256] = mm_nt(d_rows[...], weight[n : n + 256, :]).astype(bf16)
        for n, target in enumerate(r.packed):
            wait_all(target, sems.at[1 + n])

    return kernel_call(
        kernel,
        "qkv_backward",
        tables,
        dense=(d_mixed,),
        loaded=(normed, *held),
        buffers=buffers,
        outs=[ROWS_LOW],
        stored=[] if pack else [array(SHAPE[QKV], bf16)],
        packed=[array(shape, bf16) for shape in TAIL.shapes] if pack else [],
        scratch=[shape_of(QKV), pltpu.VMEM((2 * BLOCK, 1536), bf16), pltpu.SemaphoreType.DMA((7,))]
        + ([shape_of(QKV)] if pack else []),
    )


def fold(cur, axis, phase):
    half = cur.shape[0] // 2
    return add_low(cur[:half], pair_swap(cur[half:], axis, phase))


CROSS = {
    flip: [
        (device_at(z, x, c, y), device_at((z // 2) * 2 + c, x, (z % 2) ^ flip, y))
        for z in range(4)
        for x in range(4)
        for c in range(2)
        for y in range(4)
    ]
    for flip in range(2)
}
CROSS_BACK = {flip: [(b, a) for a, b in CROSS[flip]] for flip in range(2)}


def rows_to_units(halves, zl, core):
    near = lax.ppermute(jnp.where(zl == 0, halves[0], halves[1]), ALL, CROSS[0])
    far = lax.ppermute(jnp.where(zl == 0, halves[1], halves[0]), ALL, CROSS[1])
    return jnp.where(core == 0, jnp.concatenate([near, far], axis=0), jnp.concatenate([far, near], axis=0))


def units_to_rows(units, zl, core):
    near = lax.ppermute(jnp.where(core == 0, units[:8], units[8:]), ALL, CROSS_BACK[0])
    far = lax.ppermute(jnp.where(core == 0, units[8:], units[:8]), ALL, CROSS_BACK[1])
    return jnp.where(zl == 0, jnp.stack([near, far]), jnp.stack([far, near]))


def zl_swap(x):
    return lax.ppermute(x, "zl", [(0, 1), (1, 0)])


def out_to_unit(out, zl):
    low, high = out[..., :512], out[..., 512:]
    kept = jnp.where(zl == 0, low, high)
    got = zl_swap(jnp.where(zl == 0, high, low))
    return jnp.where(zl == 0, jnp.concatenate([kept, got], axis=1), jnp.concatenate([got, kept], axis=1))


def out_to_rows(units, zl):
    top, bottom = units[:, :8], units[:, 8:]
    kept = jnp.where(zl == 0, top, bottom)
    got = zl_swap(jnp.where(zl == 0, bottom, top))
    return jnp.where(zl == 0, jnp.concatenate([kept, got], axis=-1), jnp.concatenate([got, kept], axis=-1))


def body(
    tokens,
    cotangent,
    lengths,
    w_qkv,
    w_out,
    w_up,
    w_down,
    gains,
    moment_qkv,
    moment_out,
    moment_up,
    moment_down,
    moment_gains,
    square_qkv,
    square_out,
    square_up,
    square_down,
    square_gains,
):
    core = lax.axis_index("c")
    zl = lax.axis_index("zl")
    my_z = lax.axis_index("zh") * 2 + zl
    tables = unit_tables((my_z, lax.axis_index("x"), core, lax.axis_index("y")))

    both = jnp.concatenate([lengths, other_core(lengths)], axis=0)
    ends = jnp.cumsum(both, axis=-1)
    starts = ends - both
    places = jnp.arange(LENGTH, dtype=jnp.int32)
    doc_ids = jnp.sum((places[None, :, None] >= ends[:, None, :]).astype(jnp.int32), axis=-1)
    picked = doc_ids[:, :, None] == jnp.arange(4, dtype=jnp.int32)[None, None, :]
    first_place = jnp.sum(jnp.where(picked, starts[:, None, :], 0), axis=-1)
    positions = (places[None, :] - first_place).astype(f32)
    inverse = 10000.0 ** (-jnp.arange(32, dtype=f32) / 32)
    angle = positions[:, :, None] * inverse
    cos_half = jnp.cos(angle)
    sin_half = jnp.sin(angle)
    cosine = jnp.concatenate([cos_half[0], cos_half[0], cos_half[1], cos_half[1]], axis=-1)
    sine = jnp.concatenate([-sin_half[0], sin_half[0], -sin_half[1], sin_half[1]], axis=-1)
    start_rows = jnp.concatenate([first_place, jnp.zeros((6, LENGTH), jnp.int32)], axis=0)

    qkv_halves = w_qkv.astype(bf16).reshape(LAYERS, 8, 3, 4, 2, 2, 64)
    qkv_halves = qkv_halves.transpose(5, 1, 0, 3, 2, 4, 6).reshape(2, 8, LAYERS * 1536)
    up_halves = w_up.astype(bf16).reshape(LAYERS, 8, 8, 2, 256).transpose(3, 1, 0, 2, 4).reshape(2, 8, LAYERS * 2048)
    gain_rows = gains.astype(bf16).reshape(8, 8).T
    gain_rows = jnp.broadcast_to(jnp.pad(gain_rows, ((0, 0), (0, 120)))[None], (2, 8, 128))
    units = rows_to_units(jnp.concatenate([qkv_halves, up_halves, gain_rows], axis=-1), zl, core)
    qkv_units, up_units, gain_unit = units[:, :3072], units[:, 3072:7168], units[:, 7168:]
    out_units = out_to_unit(w_out.astype(bf16), zl)
    down_units = w_down.astype(bf16).reshape(LAYERS, 2, 16, 1024).transpose(0, 2, 1, 3).reshape(LAYERS, 16, 2048)
    start_space = jnp.concatenate([qkv_units[:, :1536], out_units[0], gain_unit], axis=-1)
    later_space = jnp.concatenate(
        [up_units[:, :2048], down_units[0], qkv_units[:, 1536:], out_units[1]], axis=-1
    )
    start_space = jnp.concatenate(
        [
            space[:, a:b]
            for g in range(3)
            for space, layout in ((start_space, FIRST), (later_space, SECOND))
            for a, b in layout.cuts[g]
        ],
        axis=-1,
    )
    token_rows = tokens.reshape(BLOCK, D)
    hidden = jnp.concatenate([token_rows, other_core(token_rows)], axis=0).astype(f32)
    line = jnp.concatenate([up_units[:, 2048:], down_units[1]], axis=-1)[None]
    line_got = pair_swap(line, 2, 1)
    eight = cube_all_to_all(jnp.broadcast_to(start_space[None], (8,) + start_space.shape))
    line, line_got, eight = together(line, line_got, eight)
    line = jnp.concatenate([line, line_got], axis=0)
    edges = [0]
    for g in range(3):
        edges.append(edges[-1] + FIRST.width(g) + SECOND.width(g))
    cur = [eight[..., a:b] for a, b in zip(edges, edges[1:])]
    line, line_got, got, cosine, sine, start_rows, tables, hidden = together(
        line, pair_swap(line, 2, 0), cube_round(cur, 0), cosine, sine, start_rows, tables, hidden
    )
    line = jnp.concatenate([line, line_got], axis=0)
    cur = join(cur, got)
    got = cube_round(cur, 1)
    sizes = [FIRST.width(g) for g in range(3)]
    first = join([x[..., :n] for x, n in zip(cur, sizes)], [x[..., :n] for x, n in zip(got, sizes)])
    second = join([x[..., n:] for x, n in zip(cur, sizes)], [x[..., n:] for x, n in zip(got, sizes)])
    first_got = cube_round(first, 2)
    first_got, second = together(first_got, second)
    second_got = cube_round(second, 2)
    first_buffers = [buffer for pair in zip(first, first_got) for buffer in pair]
    gains_used = gain_rows_kernel(tables, first_buffers)

    mixed, normed = qkv_forward(0, tables, gains_used, hidden, (), (FIRST, first_buffers))
    mixed, line, second_got = together(seq_swap(mixed), line, second_got)
    feed_buffer = lax.all_gather(line, XY, axis=0, tiled=True)
    second_buffers = [buffer for pair in zip(second, second_got) for buffer in pair]
    attn_source = (FIRST, first_buffers), (SECOND, second_buffers)
    feed_source = (SECOND, second_buffers), (FEED, [feed_buffer])

    turn = cosine, sine, start_rows
    previous = ()
    kept = []
    for l in range(LAYERS):
        if previous:
            mixed, normed, hidden, down_sum = qkv_forward(l, tables, gains_used, hidden, previous, attn_source[l])
            mixed = seq_swap(mixed)
        att_mine, rot, lse = att_forward(mixed, turn)
        branch, att = out_forward(tables, seq_swap(att_mine), attn_source[l])
        branch = branch, other_core(branch)
        down, branch_sum, middle, normed_mlp, active, slope = mlp_forward(
            l, tables, gains_used, branch, hidden, feed_source[l]
        )
        down = down, other_core(down)
        kept.append((hidden, normed, rot, lse, (middle, branch_sum, att), (active, slope, normed_mlp)))
        previous, hidden = down, middle
    hidden = middle[:BLOCK] + rms_norm(down[0][:BLOCK].astype(f32) + down[1][BLOCK:].astype(f32), gains_used[7:8])
    output = hidden.astype(bf16)

    grad_rows = cotangent.reshape(BLOCK, D)
    grad_rows = jnp.concatenate([grad_rows, other_core(grad_rows)], axis=0).astype(f32)
    gain_grads = jnp.zeros((8, D), f32)
    held = ()
    scattered = [None] * LAYERS
    above = ()
    for l in reversed(range(LAYERS)):
        hidden, normed, rot, lse, kept_out, kept_mlp = kept[l]
        packed, d_norm, gain_grads, *rest = mlp_backward(
            l, tables, gains_used, grad_rows, above, down, kept_mlp, feed_source[l], gain_grads
        )
        if above:
            (grad_rows,) = rest
        packed, d_norm = together(packed, d_norm)
        scattered[l] = lax.psum_scatter(packed.reshape(1024, -1), "x", scatter_dimension=0, tiled=True).reshape(16, 16, -1)
        d_norm = d_norm, other_core(d_norm)
        d_att, gain_grads, d_middle, grad_wout = out_backward(
            l, tables, gains_used, d_norm, grad_rows, kept_out, attn_source[l], gain_grads
        )
        d_mixed = seq_swap(att_backward(seq_swap(d_att), rot, lse, turn))
        d_norm, *held = qkv_backward(l, tables, d_mixed, normed, attn_source[l], (grad_wout, *held) if l == 0 else ())
        d_norm = d_norm, other_core(d_norm)
        if l == 1:
            held = held[0], grad_wout
        grad_rows = d_middle
        above = (*d_norm, hidden)
        down = (down_sum,)
    input_grad, gain_grads = last_norm(gains_used, d_norm, grad_rows, hidden, gain_grads)

    tail = [held[0], held[2]], [held[1], held[3]]
    tail = scatter_round(*tail, 2)
    feed_zero, feed_one = scattered
    feed_one = fold(feed_one, 1, 0)

    gain_sum = gain_grads.reshape(8, 128, 8).transpose(1, 0, 2).reshape(128, 1, 64)
    gain_sum = lax.all_to_all(gain_sum, ALL, 0, 0, tiled=True)
    tail, feed_one, gain_sum = together(tail, feed_one, gain_sum)
    g_gain = jnp.sum(gain_sum, axis=0).reshape(LAYERS, 4, 8)

    tail = scatter_round(*tail, 1)
    feed_one = fold(feed_one, 1, 1)
    feed_zero = fold(feed_zero, 2, 0)
    tail, feed_zero, feed_one = together(tail, feed_zero, feed_one)
    tail = scatter_round(*tail, 0)
    feed_one = fold(feed_one, 2, 0)
    feed_zero = fold(feed_zero, 2, 1)
    tail, feed_zero, feed_one = together(tail, feed_zero, feed_one)
    feed_one = fold(feed_one, 2, 1)[0]
    feed_zero = fold(fold(feed_zero, 1, 0), 1, 1)[0]
    tail_own = jnp.concatenate([jnp.concatenate(x, axis=-1) for x in tail], axis=0)
    tail_own, feed_zero, feed_one = together(cube_all_to_all(tail_own), feed_zero, feed_one)
    tail_own = jnp.sum(tail_own.astype(f32), axis=0).astype(bf16)

    g_out_units = jnp.stack([tail_own[:, 1536:2048], tail_own[:, 3584:]])
    g_down = jnp.stack([feed_zero[:, 2048:], feed_one[:, 2048:]])
    g_down = g_down.reshape(LAYERS, 16, 2, 1024).transpose(0, 2, 1, 3).reshape(LAYERS, 32, 1024).astype(f32)
    both = jnp.concatenate(
        [tail_own[:, :1536], tail_own[:, 2048:3584], feed_zero[:, :2048], feed_one[:, :2048]], axis=-1
    )
    both, g_out_units = together(both, g_out_units)
    g_out = out_to_rows(g_out_units, zl).astype(f32)
    both = units_to_rows(both, zl, core).astype(f32)
    g_qkv = both[..., :3072].reshape(2, 8, LAYERS, 4, 3, 2, 64).transpose(2, 1, 4, 3, 5, 0, 6).reshape(LAYERS, 8, 3 * D)
    g_up = both[..., 3072:].reshape(2, 8, LAYERS, 8, 256).transpose(2, 1, 3, 0, 4).reshape(LAYERS, 8, FF)

    upd_qkv = adam_update(w_qkv, moment_qkv, square_qkv, g_qkv, rate_matrix, weight_decay)
    upd_out = adam_update(w_out, moment_out, square_out, g_out, rate_matrix, weight_decay)
    upd_up = adam_update(w_up, moment_up, square_up, g_up, rate_matrix, weight_decay)
    upd_down = adam_update(w_down, moment_down, square_down, g_down, rate_matrix, weight_decay)
    upd_gains = adam_update(gains, moment_gains, square_gains, g_gain, rate_gain, 0.0)
    updates = (upd_qkv, upd_out, upd_up, upd_down, upd_gains)
    return (
        output.reshape(BLOCK, 1, D),
        input_grad.reshape(BLOCK, 1, D),
        *(u[0] for u in updates),
        *(u[1] for u in updates),
        *(u[2] for u in updates),
        *(u[0].astype(bf16) for u in updates),
    )


def solution(mesh):
    fine = Mesh(mesh.devices.reshape(2, 4, 2, 4, 2), ("zh", "x", "c", "y", "zl"))
    tokens_spec = P(SEQ, DP, None)
    rows_spec = P(None, DP + SEQ, None)
    gains_spec = P(None, None, DP + SEQ)
    masters = (rows_spec,) * 4 + (gains_spec,)
    return jax.shard_map(
        body,
        mesh=fine,
        in_specs=(tokens_spec, tokens_spec, P(DP, None)) + masters * 3,
        out_specs=(tokens_spec, tokens_spec) + masters * 4,
        check_vma=False,
    )
```
